32 devices in a mesh: section: 2 (over core), dp: 2 (over y), context: 2 (over x), tensor: 4 (over z).
Axes of the slice: x: 2, y: 2, z: 4, core: 2. Of those that a mesh axis runs over, the one named last changes fastest.
Arguments:
- inputs: bfloat16 [4, 2, 2048, 768], P(None, 'dp', ('context', 'tensor')), may hold values from -6 to 6
- cotangent: bfloat16 [4, 2, 2048, 768], P(None, 'dp', ('context', 'tensor')), may hold values from -6 to 6
- w_qkv: bfloat16 [2, 3, 768, 768], P('section', None, ('dp', 'context'), 'tensor'), may hold values from -0.21875 to 0.21875
- w_out: bfloat16 [2, 768, 768], P('section', 'tensor', ('dp', 'context')), may hold values from -2.5 to 2.5
- w_up: bfloat16 [2, 768, 3072], P('section', ('dp', 'context'), 'tensor'), may hold values from -0.21875 to 0.21875
- w_down: bfloat16 [2, 3072, 768], P('section', 'tensor', ('dp', 'context')), may hold values from -0.109375 to 0.109375
- norm_gains: bfloat16 [2, 2, 768], P('section', None, ('dp', 'context')), may hold values from 0.5 to 1.5
- norm_shifts: bfloat16 [2, 2, 768], P('section', None, ('dp', 'context')), may hold values from -1.796875 to 1.796875
Outputs:
- layer_outputs: bfloat16 [2, 4, 2, 2048, 768], P('section', None, 'dp', ('context', 'tensor'))
- boundary_grads: bfloat16 [2, 4, 2, 2048, 768], P('section', None, 'dp', ('context', 'tensor'))
- grad_w_qkv: float32 [2, 3, 768, 768], P('section', None, ('dp', 'context'), 'tensor')
- grad_w_out: float32 [2, 768, 768], P('section', 'tensor', ('dp', 'context'))
- grad_w_up: float32 [2, 768, 3072], P('section', ('dp', 'context'), 'tensor')
- grad_w_down: float32 [2, 3072, 768], P('section', 'tensor', ('dp', 'context'))
- grad_norm_gains: float32 [2, 2, 768], P('section', None, ('dp', 'context'))
- grad_norm_shifts: float32 [2, 2, 768], P('section', None, ('dp', 'context'))
The draws below stay inside these ranges and needn't reach their ends.
All inputs are finite; a program needn't handle non-finite values.
Results may differ from the reference program's by a relative error of at most 0.02.
Values may be sent and summed in bfloat16 or wider, within the bound.
No kernel may reach another device: no remote copies, remote signals or barrier semaphores. Data moves between devices by JAX's collectives and lax.ppermute only.
A program may use at most 320 MiB of HBM per device.

```python
import jax
import jax.numpy as jnp
from jax import lax

D = 768
HEADS = 12
HEAD_DIM = 64
FF = 3072
LENGTH = 2048
MICRO = 4
SEQS = 2


def level_of(key, dims, shards, smallest, high):
    def one(position, shards_of):
        draws = jax.random.uniform(jax.random.fold_in(jax.random.fold_in(key, 6), position), (shards_of,), jnp.float32, smallest / len(shards), high / len(shards))
        return jnp.repeat(jnp.exp(draws), dims[position] // shards_of).reshape((-1,) + (1,) * (len(dims) - position - 1))

    gain = one(*shards[0])
    for cut in shards[1:]:
        gain = gain * one(*cut)
    return gain


def bell_draw(own_key, shape, deviation, bound, shards=(), dtype=jnp.bfloat16):
    drawn = deviation * jax.random.normal(own_key, shape, jnp.float32)
    if shards:
        drawn = drawn * level_of(own_key, shape, shards, -0.22, 0.18)
    return jnp.clip(drawn, -bound, bound).astype(dtype)


def setup_inputs(seed: int = 0) -> dict:
    seeds = jax.random.split(jax.random.key(seed), 9)
    inputs = bell_draw(seeds[0], (MICRO, SEQS, LENGTH, D), 1.0, 6.0, ((1, 2), (2, 8)))
    cotangent = bell_draw(seeds[1], (MICRO, SEQS, LENGTH, D), 1.0, 6.0, ((1, 2), (2, 8)))
    w_qkv = bell_draw(seeds[2], (2, 3, D, D), D ** -0.5, 0.21875, ((0, 2), (2, 4), (3, 4)))
    w_out = bell_draw(seeds[3], (2, D, D), (D * 16 // LENGTH) ** -0.5, 2.5, ((0, 2), (1, 4), (2, 4)))
    w_up = bell_draw(seeds[4], (2, D, FF), D ** -0.5, 0.21875, ((0, 2), (1, 4), (2, 4)))
    w_down = bell_draw(seeds[5], (2, FF, D), FF ** -0.5, 0.109375, ((0, 2), (1, 4), (2, 4)))
    norm_gains = jnp.clip(1.0 + 0.1 * jax.random.normal(seeds[6], (2, 2, D), jnp.float32), 0.5, 1.5).astype(jnp.bfloat16)
    norm_shifts = bell_draw(seeds[7], (2, 2, D), 0.3, 1.796875, ((0, 2), (2, 4)))
    return {"inputs": inputs, "cotangent": cotangent, "w_qkv": w_qkv, "w_out": w_out, "w_up": w_up, "w_down": w_down, "norm_gains": norm_gains, "norm_shifts": norm_shifts}


EPS = 1e-05
NEG = -1e+30
HIGH = lax.Precision.HIGHEST

@jax.custom_vjp
def low(v):
    return lax.optimization_barrier(v.astype(jnp.bfloat16)).astype(jnp.float32)

@jax.custom_vjp
def low_back(v):
    return v

def low_keep(v):
    return (low(v), None)

def low_pass(kept, grad):
    return (grad,)

def back_keep(v):
    return (v, None)

def back_low(kept, grad):
    return (low(grad),)
low.defvjp(low_keep, low_pass)
low_back.defvjp(back_keep, back_low)

def normed(values, gain_row, shift_row):
    center = values - lax.optimization_barrier(jnp.mean(values, -1, keepdims=True))
    spread = lax.optimization_barrier(jnp.mean(center * center, -1, keepdims=True))
    return center * lax.rsqrt(spread + EPS) * gain_row + shift_row

def attend(pieces):
    queries, key_rows, values = pieces
    scores = jnp.einsum('qhe,khe->hqk', queries, key_rows, precision=HIGH) * HEAD_DIM ** (-0.5)
    scores = low_back(scores)
    places = jnp.arange(LENGTH)
    allowed = places[None, :] <= places[:, None]
    scores = jnp.where(allowed[None], scores, NEG)
    attention = low(jax.nn.softmax(scores, axis=-1))
    return jnp.einsum('hqk,khe->qhe', attention, values, precision=HIGH)

def layer(residual, w_qkv, w_out, w_up, w_down, norm_gain, norm_shift):
    seq_count = residual.shape[0]
    normed_a = low(normed(residual, norm_gain[0], norm_shift[0]))
    projected = jnp.einsum('nld,kde->knle', normed_a, w_qkv, precision=HIGH)
    projected = low(low_back(projected)).reshape(3, seq_count, LENGTH, HEADS, HEAD_DIM)
    mixture = lax.map(jax.checkpoint(attend), (projected[0], projected[1], projected[2]))
    mixture = low(low_back(mixture.reshape(seq_count, LENGTH, D)))
    attended = low_back(jnp.einsum('nld,de->nle', mixture, w_out, precision=HIGH))
    hidden = residual + attended
    normed_b = low(normed(hidden, norm_gain[1], norm_shift[1]))
    pre_act = low_back(jnp.einsum('nld,df->nlf', normed_b, w_up, precision=HIGH))
    activated = low(jax.nn.gelu(pre_act))
    branch = low_back(jnp.einsum('nlf,fd->nld', activated, w_down, precision=HIGH))
    return hidden + branch

def reference(inputs, cotangent, w_qkv, w_out, w_up, w_down, norm_gains, norm_shifts):
    pair_count = MICRO * SEQS // 2
    first_in = inputs.reshape(pair_count, 2, LENGTH, D)
    top_grad = cotangent.reshape(pair_count, 2, LENGTH, D)
    stacked = (w_qkv, w_out, w_up, w_down, norm_gains, norm_shifts)
    layer_zero = tuple((weight[0].astype(jnp.float32) for weight in stacked))
    layer_one = tuple((weight[1].astype(jnp.float32) for weight in stacked))

    def per_pair(running, pieces):
        entries, outer_grad = pieces
        first_out, first_back = jax.vjp(layer, entries.astype(jnp.float32), *layer_zero)
        handed = first_out.astype(jnp.bfloat16)
        second_out, second_back = jax.vjp(layer, handed.astype(jnp.float32), *layer_one)
        second_grads = second_back(outer_grad.astype(jnp.float32))
        handed_grad = second_grads[0].astype(jnp.bfloat16)
        first_grads = first_back(handed_grad.astype(jnp.float32))
        running = tuple((total_sum + jnp.stack([early, later]) for total_sum, early, later in zip(running, first_grads[1:], second_grads[1:])))
        return (running, (handed, second_out.astype(jnp.bfloat16), first_grads[0].astype(jnp.bfloat16), handed_grad))
    zeros_init = tuple((jnp.zeros(weight.shape, jnp.float32) for weight in stacked))
    totals, (outs_zero, outs_one, grads_zero, grads_one) = lax.scan(per_pair, zeros_init, (first_in, top_grad))
    full_shape = (MICRO, SEQS, LENGTH, D)
    layer_outputs = jnp.stack([outs_zero.reshape(full_shape), outs_one.reshape(full_shape)])
    boundary_grads = jnp.stack([grads_zero.reshape(full_shape), grads_one.reshape(full_shape)])
    return (layer_outputs, boundary_grads, totals[0], totals[1], totals[2], totals[3], totals[4], totals[5])
```

```python
import functools

import jax
import jax.numpy as jnp
from jax import lax
from jax.experimental import pallas as pl
from jax.experimental.pallas import tpu as pltpu
from jax.sharding import PartitionSpec as P

HEAD_DIM = 64
EPS = 1e-05
NEG = -1e30
BLOCK = 512
SCALE = HEAD_DIM ** (-0.5)
F32 = jnp.float32
BF16 = jnp.bfloat16
VMEM_LIMIT = 48 * 1024 * 1024


def normed(values, gain_row, shift_row):
    center = values - jnp.mean(values, -1, keepdims=True)
    spread = jnp.mean(center * center, -1, keepdims=True)
    return center * lax.rsqrt(spread + EPS) * gain_row + shift_row


def dot(left, right, contract):
    return lax.dot_general(left, right, ((contract[0], contract[1]), ((), ())),
                           preferred_element_type=F32)


def attend_kernel(block, heads, rows_ref, all_ref, mix_ref, log_ref):
    place = pl.program_id(0)
    width = heads * HEAD_DIM
    row_ids = lax.broadcasted_iota(jnp.int32, (block, block), 0)
    col_ids = lax.broadcasted_iota(jnp.int32, (block, block), 1)
    for head in range(heads):
        low = head * HEAD_DIM
        queries = rows_ref[:, low:low + HEAD_DIM] * jnp.asarray(SCALE, BF16)

        def step(index, carry, masked):
            top, total, mixed = carry
            span = pl.ds(pl.multiple_of(index * block, block), block)
            keys = all_ref[span, width + low:width + low + HEAD_DIM]
            values = all_ref[span, 2 * width + low:2 * width + low + HEAD_DIM]
            scores = dot(queries, keys, ((1,), (1,)))
            if masked:
                scores = jnp.where(col_ids <= row_ids, scores, NEG)
            new_top = jnp.maximum(top, jnp.max(scores, -1, keepdims=True))
            grown = jnp.exp(scores - new_top)
            shrink = jnp.exp(top - new_top)
            return (
                new_top,
                total * shrink + jnp.sum(grown, -1, keepdims=True),
                mixed * shrink + dot(grown.astype(BF16), values, ((1,), (0,))),
            )

        carry = (
            jnp.full((block, 1), NEG, F32),
            jnp.zeros((block, 1), F32),
            jnp.zeros((block, HEAD_DIM), F32),
        )
        carry = lax.fori_loop(0, place, lambda i, c: step(i, c, False), carry)
        top, total, mixed = step(place, carry, True)
        mix_ref[:, low:low + HEAD_DIM] = (mixed / total).astype(BF16)
        wide = jnp.broadcast_to(top + jnp.log(total), (block, 128))
        log_ref[head] = wide.T[:1]


def attend(packed, heads):
    length, width = packed.shape
    block = min(BLOCK, length)
    return pl.pallas_call(
        functools.partial(attend_kernel, block, heads),
        grid=(length // block,),
        in_specs=[
            pl.BlockSpec((block, width), lambda i: (i, 0)),
            pl.BlockSpec((length, width), lambda i: (0, 0)),
        ],
        out_specs=[
            pl.BlockSpec((block, width // 3), lambda i: (i, 0)),
            pl.BlockSpec((heads, 1, block), lambda i: (0, 0, i)),
        ],
        out_shape=[
            jax.ShapeDtypeStruct((length, width // 3), BF16),
            jax.ShapeDtypeStruct((heads, 1, length), F32),
        ],
        compiler_params=pltpu.CompilerParams(vmem_limit_bytes=VMEM_LIMIT),
        cost_estimate=pl.CostEstimate(
            flops=2 * 2 * length * length * HEAD_DIM * heads,
            bytes_accessed=length * width * 4,
            transcendentals=length * length * heads // 2,
        ),
        name="attend",
    )(packed, packed)


def attend_back_kernel(block, heads, rows_ref, all_ref, grad_ref, mix_ref, log_ref, out_ref,
                       query_sum, inner):
    place = pl.program_id(0)
    count = pl.num_programs(0)
    width = heads * HEAD_DIM
    key_ids = lax.broadcasted_iota(jnp.int32, (block, block), 0)
    query_ids = lax.broadcasted_iota(jnp.int32, (block, block), 1)

    @pl.when(place == 0)
    def prepare():
        query_sum[...] = jnp.zeros_like(query_sum)

        def one(index, carry):
            span = pl.ds(pl.multiple_of(index * block, block), block)
            product = grad_ref[span, :].astype(F32) * mix_ref[span, :].astype(F32)
            for head in range(heads):
                part = product[:, head * HEAD_DIM:(head + 1) * HEAD_DIM]
                inner[head, :, span] = jnp.sum(part.T, 0, keepdims=True)
            return carry

        lax.fori_loop(0, count, one, 0)

    for head in range(heads):
        low = head * HEAD_DIM
        keys = rows_ref[:, width + low:width + low + HEAD_DIM] * jnp.asarray(SCALE, BF16)
        values = rows_ref[:, 2 * width + low:2 * width + low + HEAD_DIM]

        def step(index, carry, masked):
            key_sum, value_sum = carry
            span = pl.ds(pl.multiple_of(index * block, block), block)
            queries = all_ref[span, low:low + HEAD_DIM]
            grads = grad_ref[span, low:low + HEAD_DIM]
            scores = dot(keys, queries, ((1,), (1,)))
            if masked:
                scores = jnp.where(key_ids <= query_ids, scores, NEG)
            probs = jnp.exp(scores - log_ref[head, :, span])
            grad_probs = dot(values, grads, ((1,), (1,)))
            grad_scores = (probs * (grad_probs - inner[head, :, span])).astype(BF16)
            value_sum = value_sum + dot(probs.astype(BF16), grads, ((1,), (0,)))
            key_sum = key_sum + dot(grad_scores, queries, ((1,), (0,)))
            query_sum[head, span, :] += dot(grad_scores, keys, ((0,), (0,)))
            return key_sum, value_sum

        carry = (jnp.zeros((block, HEAD_DIM), F32), jnp.zeros((block, HEAD_DIM), F32))
        carry = step(place, carry, True)
        key_sum, value_sum = lax.fori_loop(
            place + 1, count, lambda i, c: step(i, c, False), carry)
        own = pl.ds(pl.multiple_of(place * block, block), block)
        out_ref[:, low:low + HEAD_DIM] = query_sum[head, own, :].astype(BF16)
        out_ref[:, width + low:width + low + HEAD_DIM] = (key_sum * SCALE).astype(BF16)
        out_ref[:, 2 * width + low:2 * width + low + HEAD_DIM] = value_sum.astype(BF16)


def attend_back(packed, grads, mixture, logs, heads):
    length, width = packed.shape
    block = min(BLOCK, length)
    third = width // 3
    return pl.pallas_call(
        functools.partial(attend_back_kernel, block, heads),
        grid=(length // block,),
        in_specs=[
            pl.BlockSpec((block, width), lambda i: (i, 0)),
            pl.BlockSpec((length, width), lambda i: (0, 0)),
            pl.BlockSpec((length, third), lambda i: (0, 0)),
            pl.BlockSpec((length, third), lambda i: (0, 0)),
            pl.BlockSpec((heads, 1, length), lambda i: (0, 0, 0)),
        ],
        out_specs=pl.BlockSpec((block, width), lambda i: (i, 0)),
        out_shape=jax.ShapeDtypeStruct((length, width), BF16),
        scratch_shapes=[
            pltpu.VMEM((heads, length, HEAD_DIM), F32),
            pltpu.VMEM((heads, 1, length), F32),
        ],
        compiler_params=pltpu.CompilerParams(vmem_limit_bytes=VMEM_LIMIT),
        cost_estimate=pl.CostEstimate(
            flops=2 * 5 * length * length * HEAD_DIM * heads,
            bytes_accessed=length * width * 8,
            transcendentals=length * length * heads // 2,
        ),
        name="attend_back",
    )(packed, packed, grads, mixture, logs)


def swap(value, axis):
    return lax.ppermute(value, axis, [(0, 1), (1, 0)])


def put(buffer, value, places):
    starts = [0 if place is None else place for place in places]
    starts += [0] * (buffer.ndim - len(starts))
    shape = [buffer.shape[n] if n >= len(places) or places[n] is None else 1
             for n in range(buffer.ndim)]
    return lax.dynamic_update_slice(buffer, value.reshape(shape), starts)


def take(buffer, index, axis=0):
    return lax.dynamic_index_in_dim(buffer, index, axis, keepdims=False)


def line_gather(value, axis):
    count = lax.axis_size(axis)
    place = lax.axis_index(axis)
    up = [(n, n + 1) for n in range(count - 1)]
    down = [(n + 1, n) for n in range(count - 1)]
    from_low, from_high = [value], [value]
    for step in range(1, count):
        from_low.append(lax.ppermute(from_low[-1], axis, up))
        from_high.append(lax.ppermute(from_high[-1], axis, down))
    gathered = jnp.zeros((count,) + value.shape, value.dtype)
    gathered = put(gathered, value, (place,))
    for step in range(1, count):
        piece = from_high[step] + from_low[count - step]
        gathered = put(gathered, piece, (lax.rem(place + step, count),))
    return gathered


def line_reduce(blocks, axis):
    count = lax.axis_size(axis)
    place = lax.axis_index(axis)
    up = [(n, n + 1) for n in range(count - 1)]
    down = [(n + 1, n) for n in range(count - 1)]
    rising = falling = None
    for step in range(1, count):
        ahead = take(blocks, jnp.minimum(place + count - step, count - 1))
        behind = take(blocks, jnp.maximum(place - count + step, 0))
        if rising is not None:
            ahead = (ahead.astype(F32) + rising.astype(F32)).astype(BF16)
            behind = (behind.astype(F32) + falling.astype(F32)).astype(BF16)
        rising = lax.ppermute(ahead, axis, up)
        falling = lax.ppermute(behind, axis, down)
    return take(blocks, place).astype(F32) + rising.astype(F32) + falling.astype(F32)


def spread_tensor(blocks):
    count = lax.axis_size("tensor")
    place = lax.axis_index("tensor")
    result = put(jnp.zeros_like(blocks), take(blocks, place), (place,))
    for step in range(1, count):
        pairs = [(n, (n + step) % count) for n in range(count)]
        piece = lax.ppermute(take(blocks, lax.rem(place + step, count)), "tensor", pairs)
        result = put(result, piece, (lax.rem(place + count - step, count),))
    return result


def group_pairs(count, step):
    return [(n, n ^ step) for n in range(count)]


GROUP = ("section", "context")


def to_heads(blocks):
    count = blocks.shape[0]
    sections = lax.axis_size("section")
    contexts = count // sections
    place = lax.axis_index("section") * contexts + lax.axis_index("context")
    result = jnp.zeros((contexts, blocks.shape[1], sections) + blocks.shape[2:],
                       blocks.dtype)
    for step in range(count):
        other = lax.bitwise_xor(place, step)
        piece = take(blocks, other)
        if step:
            piece = lax.ppermute(piece, GROUP, group_pairs(count, step))
        result = put(result, piece, (lax.rem(other, contexts), None, other // contexts))
    return result


def from_heads(spread):
    contexts, _, sections = spread.shape[:3]
    count = contexts * sections
    place = lax.axis_index("section") * contexts + lax.axis_index("context")
    result = jnp.zeros((count,) + spread.shape[1:2] + spread.shape[3:], spread.dtype)
    for step in range(count):
        other = lax.bitwise_xor(place, step)
        piece = take(take(spread, lax.rem(other, contexts)), other // contexts, 1)
        if step:
            piece = lax.ppermute(piece, GROUP, group_pairs(count, step))
        result = put(result, piece, (other,))
    return result


def gather_rows(half):
    section = lax.axis_index("section")
    sections = lax.axis_size("section")
    dp_count, ctx_count = lax.axis_size("dp"), lax.axis_size("context")
    rows, width = half.shape
    if dp_count == 2 and ctx_count == 2 and rows % 2 == 0:
        dp, ctx = lax.axis_index("dp"), lax.axis_index("context")
        first, second = half[:rows // 2], half[rows // 2:]
        pair_shape = (2,) + first.shape
        near = put(jnp.zeros(pair_shape, half.dtype), first, (ctx,))
        near = put(near, swap(first, "context"), (1 - ctx,))
        other = put(jnp.zeros(pair_shape, half.dtype), second, (dp,))
        other = put(other, swap(second, "dp"), (1 - dp,))
        near_far, other_far = swap(near, "dp"), swap(other, "context")
        whole = jnp.zeros((2, 2, sections, 2, rows // 2, width), half.dtype)
        for value, places in (
            (near, (dp, None, None, 0)),
            (other, (None, ctx, None, 1)),
            (near_far, (1 - dp, None, None, 0)),
            (other_far, (None, 1 - ctx, None, 1)),
        ):
            for held, where in ((value, section), (swap(value, "section"), 1 - section)):
                whole = put(whole, held, (places[0], places[1], where, places[3]))
    else:
        gathered = lax.all_gather(half, ("dp", "context"))
        whole = jnp.zeros((dp_count * ctx_count, sections, rows, width), half.dtype)
        whole = put(whole, gathered, (None, section))
        whole = put(whole, swap(gathered, "section"), (None, 1 - section))
    return whole.reshape(-1, width)


def add_bf16(left, right):
    return (left.astype(F32) + right.astype(F32)).astype(BF16)


def reduce_rows(partial):
    section = lax.axis_index("section")
    sections = lax.axis_size("section")
    dp_count, ctx_count = lax.axis_size("dp"), lax.axis_size("context")
    width = partial.shape[1]
    rows = partial.shape[0] // (dp_count * ctx_count * sections)
    if dp_count == 2 and ctx_count == 2 and rows % 2 == 0:
        dp, ctx = lax.axis_index("dp"), lax.axis_index("context")
        split = partial.reshape(2, 2, sections, rows, width)
        mine = add_bf16(take(split, section, 2), swap(take(split, 1 - section, 2), "section"))
        first, second = mine[:, :, :rows // 2], mine[:, :, rows // 2:]
        first = add_bf16(take(first, dp), swap(take(first, 1 - dp), "dp"))
        second = add_bf16(take(second, ctx, 1), swap(take(second, 1 - ctx, 1), "context"))
        first = add_bf16(take(first, ctx), swap(take(first, 1 - ctx), "context"))
        second = add_bf16(take(second, dp), swap(take(second, 1 - dp), "dp"))
        return jnp.concatenate([first, second])
    split = partial.reshape(-1, sections, rows, width)
    mine = add_bf16(take(split, section, 1), swap(take(split, 1 - section, 1), "section"))
    return lax.psum_scatter(mine, ("dp", "context"), scatter_dimension=0)


def per_device(inputs, cotangent, w_qkv, w_out, w_up, w_down, norm_gains, norm_shifts):
    section = lax.axis_index("section")
    tensors = lax.axis_size("tensor")
    sections = lax.axis_size("section")
    contexts = lax.axis_size("context")
    groups = contexts * sections
    micro, _, span, width = inputs.shape
    assert micro == tensors and sections == 2
    rows = span // sections
    count = tensors * rows
    head_total = width // HEAD_DIM
    heads = -(-head_total // groups)

    slabs = [
        w_qkv[0].transpose(1, 0, 2).reshape(w_qkv.shape[2], -1),
        w_out[0].T,
        w_up[0],
        w_down[0].T,
    ]
    norms = jnp.concatenate([norm_gains[0], norm_shifts[0]]).T
    widths = [slab.shape[1] for slab in slabs]
    slab = jnp.concatenate(slabs + [norms], 1)
    split = slab.reshape(sections, -1, slab.shape[1])
    kept = take(split, section)
    came = swap(take(split, 1 - section), "section")
    half_rows = kept.shape[0]

    def gather_layer(layer):
        half = jnp.where(section == layer, kept, came)
        starts = [sum(widths[:n]) for n in range(5)]
        parts = [half[:, starts[n]:starts[n + 1]] for n in range(4)]
        norm_part = half[:, starts[4]:]
        result = []
        for members in ((0,), (1, 2), (3,)):
            joined = parts[members[0]] if len(members) == 1 else jnp.concatenate(
                [parts[n] for n in members], 1)
            lined = line_gather(joined, "tensor")
            columns, place = [], 0
            for n in members:
                piece = lined[:, :, place:place + widths[n]]
                columns.append(piece.transpose(1, 0, 2).reshape(half_rows, -1))
                place += widths[n]
            if members == (0,):
                columns.append(norm_part)
            sizes = [column.shape[1] for column in columns]
            full = gather_rows(jnp.concatenate(columns, 1) if len(columns) > 1 else columns[0])
            place = 0
            for size in sizes:
                result.append(full[:, place:place + size])
                place += size
        qkv, norm_rows, out, up, down = result
        norm_rows = norm_rows.T.astype(F32)
        return qkv, out, up, down, norm_rows[:2], norm_rows[2:]

    def to_groups(projected):
        if groups == tensors:
            blocks = projected.reshape(tensors, rows, groups, -1)
        else:
            shaped = projected.reshape(count, tensors, 3, -1, HEAD_DIM)
            shaped = shaped.transpose(0, 2, 1, 3, 4).reshape(count, 3, head_total, HEAD_DIM)
            shaped = jnp.pad(shaped, ((0, 0), (0, 0), (0, groups * heads - head_total), (0, 0)))
            shaped = shaped.reshape(count, 3, groups, -1).transpose(0, 2, 1, 3)
            blocks = shaped.reshape(tensors, rows, groups, -1)
        return blocks.transpose(2, 0, 1, 3)

    def from_groups(blocks):
        shaped = blocks.transpose(1, 2, 0, 3)
        if groups == tensors:
            return shaped.reshape(count, -1)
        shaped = shaped.reshape(count, groups, 3, heads * HEAD_DIM).transpose(0, 2, 1, 3)
        shaped = shaped.reshape(count, 3, -1)[:, :, :width]
        return shaped.reshape(count, 3, tensors, -1).transpose(0, 2, 1, 3).reshape(count, -1)

    def mix_to_groups(mixed):
        pad = groups * heads * HEAD_DIM - width
        if pad:
            mixed = jnp.pad(mixed, ((0, 0), (0, pad)))
        return mixed.reshape(tensors, rows, groups, -1).transpose(2, 0, 1, 3)

    def mix_from_groups(blocks):
        return blocks.transpose(1, 2, 0, 3).reshape(count, -1)[:, :width]

    def spread_heads(blocks):
        spread = to_heads(blocks)
        return spread.reshape(-1, spread.shape[-1])

    def collect_heads(flat):
        return from_heads(flat.reshape(contexts, tensors, sections, rows, -1))

    def forward(layer_in, weights):
        qkv, out, up, down, gains, shifts = weights
        residual = layer_in.astype(F32)
        normed_a = normed(residual, gains[0], shifts[0]).astype(BF16)
        projected = dot(normed_a, qkv, ((1,), (0,))).astype(BF16)
        packed = spread_heads(to_groups(projected))
        mixed, logs = attend(packed, heads)
        mixture = mix_from_groups(collect_heads(mixed))
        hidden = residual + dot(mixture, out, ((1,), (1,)))
        normed_b = normed(hidden, gains[1], shifts[1]).astype(BF16)
        pre_act = dot(normed_b, up, ((1,), (0,)))
        activated = jax.nn.gelu(pre_act).astype(BF16)
        layer_out = hidden + dot(activated, down, ((1,), (1,)))
        saved = (residual, normed_a, packed, mixed, logs, mixture, hidden, normed_b, pre_act)
        return layer_out.astype(BF16), saved

    def backward(grad_in, saved, weights):
        qkv, out, up, down, gains, shifts = weights
        residual, normed_a, packed, mixed, logs, mixture, hidden, normed_b, pre_act = saved
        grad_branch = grad_in.astype(BF16)
        grad_in = grad_in.astype(F32)
        grad_act = dot(grad_branch, down, ((1,), (0,)))
        activated, gelu_back = jax.vjp(jax.nn.gelu, pre_act)
        grad_pre = gelu_back(grad_act)[0].astype(BF16)
        grad_down = dot(grad_branch, activated.astype(BF16), ((0,), (0,))).astype(BF16)
        grad_up = dot(normed_b, grad_pre, ((0,), (0,))).astype(BF16)
        grad_second = dot(grad_pre, up, ((1,), (1,)))
        _, second_back = jax.vjp(normed, hidden, gains[1], shifts[1])
        grad_hidden_norm, gain_later, shift_later = second_back(grad_second)
        grad_hidden = grad_in + grad_hidden_norm
        grad_attn = grad_hidden.astype(BF16)
        grad_out = dot(grad_attn, mixture, ((0,), (0,))).astype(BF16)
        grad_mixture = dot(grad_attn, out, ((1,), (0,))).astype(BF16)
        grad_mixed = spread_heads(mix_to_groups(grad_mixture))
        grad_packed = attend_back(packed, grad_mixed, mixed, logs, heads)
        grad_proj = from_groups(collect_heads(grad_packed))
        grad_qkv = dot(normed_a, grad_proj, ((0,), (0,))).astype(BF16)
        grad_first = dot(grad_proj, qkv, ((1,), (1,)))
        _, first_back = jax.vjp(normed, residual, gains[0], shifts[0])
        grad_input_norm, gain_early, shift_early = first_back(grad_first)
        grad_input = (grad_hidden + grad_input_norm).astype(BF16)
        grad_norms = jnp.stack([gain_early, gain_later, shift_early, shift_later], 1)
        return grad_input, (grad_qkv, grad_out, grad_up, grad_down, grad_norms)

    def reduce_layer(grads):
        grad_qkv, grad_out, grad_up, grad_down, grad_norms = grads
        result = []
        for members in ((grad_down,), (grad_out, grad_up), (grad_qkv, grad_norms)):
            joined = jnp.concatenate([part.astype(BF16) for part in members], 1)
            joined = reduce_rows(joined)
            blocks, place = [], 0
            for part in members:
                size = part.shape[1]
                piece = joined[:, place:place + size]
                place += size
                if part is grad_norms:
                    blocks.append(jnp.broadcast_to(piece, (tensors,) + piece.shape))
                else:
                    blocks.append(piece.reshape(half_rows, tensors, -1).transpose(1, 0, 2))
            total = line_reduce(jnp.concatenate(blocks, 2), "tensor")
            place = 0
            for block in blocks:
                result.append(total[:, place:place + block.shape[2]])
                place += block.shape[2]
        down, out, up, qkv, norms = result
        return jnp.concatenate([qkv, out, up, down, norms], 1).astype(BF16)

    def own_rows(value):
        half = take(value.reshape(micro, sections, rows, width), section, 1)
        return spread_tensor(half).reshape(count, width)

    def back_rows(value):
        return spread_tensor(value.reshape(tensors, rows, width))

    def place_layers(lower, upper):
        keep = jnp.where(section == 0, lower, upper)
        came_rows = swap(jnp.where(section == 0, upper, lower), "section")
        whole = jnp.zeros((micro, sections, rows, width), BF16)
        whole = put(whole, keep, (None, section))
        whole = put(whole, came_rows, (None, 1 - section))
        return whole.reshape(1, micro, 1, span, width)

    entries = own_rows(inputs)
    weights_zero = gather_layer(0)
    weights_one = gather_layer(1)
    top_grad = own_rows(cotangent)
    out_zero, saved_zero = forward(entries, weights_zero)
    out_one, saved_one = forward(out_zero, weights_one)
    layer_outputs = place_layers(back_rows(out_zero), back_rows(out_one))
    grad_one, grads_one = backward(top_grad, saved_one, weights_one)
    reduced_one = reduce_layer(grads_one)
    grad_zero, grads_zero = backward(grad_one, saved_zero, weights_zero)
    boundary_grads = place_layers(back_rows(grad_zero), back_rows(grad_one))
    reduced_zero = reduce_layer(grads_zero)

    keep = jnp.where(section == 0, reduced_zero, reduced_one)
    came_half = swap(jnp.where(section == 0, reduced_one, reduced_zero), "section")
    total = jnp.zeros((sections,) + keep.shape, BF16)
    total = put(total, keep, (section,))
    total = put(total, came_half, (1 - section,))
    total = total.reshape(-1, keep.shape[1]).astype(F32)
    starts = [sum(widths[:n]) for n in range(5)]
    grad_qkv, grad_out, grad_up, grad_down = (
        total[:, starts[n]:starts[n + 1]] for n in range(4))
    norms = total[:, starts[4]:].T
    return (
        layer_outputs,
        boundary_grads,
        grad_qkv.reshape(grad_qkv.shape[0], 3, -1).transpose(1, 0, 2)[None],
        grad_out.T[None],
        grad_up[None],
        grad_down.T[None],
        norms[:2][None],
        norms[2:][None],
    )


def solution(mesh):
    in_specs = (
        P(None, "dp", ("context", "tensor"), None),
        P(None, "dp", ("context", "tensor"), None),
        P("section", None, ("dp", "context"), "tensor"),
        P("section", "tensor", ("dp", "context")),
        P("section", ("dp", "context"), "tensor"),
        P("section", "tensor", ("dp", "context")),
        P("section", None, ("dp", "context")),
        P("section", None, ("dp", "context")),
    )
    out_specs = (
        P("section", None, "dp", ("context", "tensor"), None),
        P("section", None, "dp", ("context", "tensor"), None),
        P("section", None, ("dp", "context"), "tensor"),
        P("section", "tensor", ("dp", "context")),
        P("section", ("dp", "context"), "tensor"),
        P("section", "tensor", ("dp", "context")),
        P("section", None, ("dp", "context")),
        P("section", None, ("dp", "context")),
    )
    return jax.shard_map(
        per_device, mesh=mesh, in_specs=in_specs, out_specs=out_specs, check_vma=False
    )
```

```python
import functools

import jax
import jax.numpy as jnp
from jax import lax
from jax.experimental import pallas as pl
from jax.experimental.pallas import tpu as pltpu
from jax.experimental.layout import Layout, with_layout_constraint
from jax.sharding import PartitionSpec as P

HEAD_DIM = 64
EPS = 1e-05
NEG = -1e30
BLOCK = 512
SCALE = HEAD_DIM ** (-0.5)
F32 = jnp.float32
BF16 = jnp.bfloat16
VMEM_LIMIT = 48 * 1024 * 1024


def normed(values, gain_row, shift_row):
    center = values - jnp.mean(values, -1, keepdims=True)
    spread = jnp.mean(center * center, -1, keepdims=True)
    return center * lax.rsqrt(spread + EPS) * gain_row + shift_row


def dot(left, right, contract):
    return lax.dot_general(left, right, ((contract[0], contract[1]), ((), ())),
                           preferred_element_type=F32)


def attend_kernel(block, heads, rows_ref, all_ref, mix_ref, log_ref):
    place = pl.program_id(0)
    width = heads * HEAD_DIM
    row_ids = lax.broadcasted_iota(jnp.int32, (block, block), 0)
    col_ids = lax.broadcasted_iota(jnp.int32, (block, block), 1)
    for head in range(heads):
        low = head * HEAD_DIM
        queries = rows_ref[:, low:low + HEAD_DIM] * jnp.asarray(SCALE, BF16)

        def step(index, carry, masked):
            top, total, mixed = carry
            span = pl.ds(pl.multiple_of(index * block, block), block)
            keys = all_ref[span, width + low:width + low + HEAD_DIM]
            values = all_ref[span, 2 * width + low:2 * width + low + HEAD_DIM]
            scores = dot(queries, keys, ((1,), (1,)))
            if masked:
                scores = jnp.where(col_ids <= row_ids, scores, NEG)
            new_top = jnp.maximum(top, jnp.max(scores, -1, keepdims=True))
            grown = jnp.exp(scores - new_top)
            shrink = jnp.exp(top - new_top)
            return (
                new_top,
                total * shrink + jnp.sum(grown, -1, keepdims=True),
                mixed * shrink + dot(grown.astype(BF16), values, ((1,), (0,))),
            )

        carry = (
            jnp.full((block, 1), NEG, F32),
            jnp.zeros((block, 1), F32),
            jnp.zeros((block, HEAD_DIM), F32),
        )
        carry = lax.fori_loop(0, place, lambda i, c: step(i, c, False), carry)
        top, total, mixed = step(place, carry, True)
        mix_ref[:, low:low + HEAD_DIM] = (mixed / total).astype(BF16)
        wide = jnp.broadcast_to(top + jnp.log(total), (block, 128))
        log_ref[head] = wide.T[:1]


def attend(packed, heads):
    length, width = packed.shape
    block = min(BLOCK, length)
    return pl.pallas_call(
        functools.partial(attend_kernel, block, heads),
        grid=(length // block,),
        in_specs=[
            pl.BlockSpec((block, width), lambda i: (i, 0)),
            pl.BlockSpec((length, width), lambda i: (0, 0)),
        ],
        out_specs=[
            pl.BlockSpec((block, width // 3), lambda i: (i, 0)),
            pl.BlockSpec((heads, 1, block), lambda i: (0, 0, i)),
        ],
        out_shape=[
            jax.ShapeDtypeStruct((length, width // 3), BF16),
            jax.ShapeDtypeStruct((heads, 1, length), F32),
        ],
        compiler_params=pltpu.CompilerParams(vmem_limit_bytes=VMEM_LIMIT),
        cost_estimate=pl.CostEstimate(
            flops=2 * 2 * length * length * HEAD_DIM * heads,
            bytes_accessed=length * width * 4,
            transcendentals=length * length * heads // 2,
        ),
        name="attend",
    )(packed, packed)


def attend_back_kernel(block, heads, rows_ref, all_ref, grad_ref, mix_ref, log_ref, out_ref,
                       query_sum, inner):
    place = pl.program_id(0)
    count = pl.num_programs(0)
    width = heads * HEAD_DIM
    key_ids = lax.broadcasted_iota(jnp.int32, (block, block), 0)
    query_ids = lax.broadcasted_iota(jnp.int32, (block, block), 1)

    @pl.when(place == 0)
    def prepare():
        query_sum[...] = jnp.zeros_like(query_sum)

        def one(index, carry):
            span = pl.ds(pl.multiple_of(index * block, block), block)
            product = grad_ref[span, :].astype(F32) * mix_ref[span, :].astype(F32)
            for head in range(heads):
                part = product[:, head * HEAD_DIM:(head + 1) * HEAD_DIM]
                inner[head, :, span] = jnp.sum(part.T, 0, keepdims=True)
            return carry

        lax.fori_loop(0, count, one, 0)

    for head in range(heads):
        low = head * HEAD_DIM
        keys = rows_ref[:, width + low:width + low + HEAD_DIM] * jnp.asarray(SCALE, BF16)
        values = rows_ref[:, 2 * width + low:2 * width + low + HEAD_DIM]

        def step(index, carry, masked):
            key_sum, value_sum = carry
            span = pl.ds(pl.multiple_of(index * block, block), block)
            queries = all_ref[span, low:low + HEAD_DIM]
            grads = grad_ref[span, low:low + HEAD_DIM]
            scores = dot(keys, queries, ((1,), (1,)))
            if masked:
                scores = jnp.where(key_ids <= query_ids, scores, NEG)
            probs = jnp.exp(scores - log_ref[head, :, span])
            grad_probs = dot(values, grads, ((1,), (1,)))
            grad_scores = (probs * (grad_probs - inner[head, :, span])).astype(BF16)
            value_sum = value_sum + dot(probs.astype(BF16), grads, ((1,), (0,)))
            key_sum = key_sum + dot(grad_scores, queries, ((1,), (0,)))
            query_sum[head, span, :] += dot(grad_scores, keys, ((0,), (0,)))
            return key_sum, value_sum

        carry = (jnp.zeros((block, HEAD_DIM), F32), jnp.zeros((block, HEAD_DIM), F32))
        carry = step(place, carry, True)
        key_sum, value_sum = lax.fori_loop(
            place + 1, count, lambda i, c: step(i, c, False), carry)
        own = pl.ds(pl.multiple_of(place * block, block), block)
        out_ref[:, low:low + HEAD_DIM] = query_sum[head, own, :].astype(BF16)
        out_ref[:, width + low:width + low + HEAD_DIM] = (key_sum * SCALE).astype(BF16)
        out_ref[:, 2 * width + low:2 * width + low + HEAD_DIM] = value_sum.astype(BF16)


def attend_back(packed, grads, mixture, logs, heads):
    length, width = packed.shape
    block = min(BLOCK, length)
    third = width // 3
    return pl.pallas_call(
        functools.partial(attend_back_kernel, block, heads),
        grid=(length // block,),
        in_specs=[
            pl.BlockSpec((block, width), lambda i: (i, 0)),
            pl.BlockSpec((length, width), lambda i: (0, 0)),
            pl.BlockSpec((length, third), lambda i: (0, 0)),
            pl.BlockSpec((length, third), lambda i: (0, 0)),
            pl.BlockSpec((heads, 1, length), lambda i: (0, 0, 0)),
        ],
        out_specs=pl.BlockSpec((block, width), lambda i: (i, 0)),
        out_shape=jax.ShapeDtypeStruct((length, width), BF16),
        scratch_shapes=[
            pltpu.VMEM((heads, length, HEAD_DIM), F32),
            pltpu.VMEM((heads, 1, length), F32),
        ],
        compiler_params=pltpu.CompilerParams(vmem_limit_bytes=VMEM_LIMIT),
        cost_estimate=pl.CostEstimate(
            flops=2 * 5 * length * length * HEAD_DIM * heads,
            bytes_accessed=length * width * 8,
            transcendentals=length * length * heads // 2,
        ),
        name="attend_back",
    )(packed, packed, grads, mixture, logs)


def swap(value, axis):
    return lax.ppermute(value, axis, [(0, 1), (1, 0)])


def take(buffer, index, axis=0):
    return lax.dynamic_index_in_dim(buffer, index, axis, keepdims=False)


def paired(near, far, place, axis):
    first = jnp.where(place == 0, near, far)
    second = jnp.where(place == 0, far, near)
    return jnp.concatenate([first, second], axis)


def in_order(blocks, place):
    if len(blocks) == 2:
        return paired(blocks[0][None], blocks[1][None], place, 0)
    stacked = jnp.zeros((len(blocks),) + blocks[0].shape, blocks[0].dtype)
    for step, block in enumerate(blocks):
        stacked = lax.dynamic_update_index_in_dim(
            stacked, block, lax.bitwise_xor(place, step), 0)
    return stacked


def hold(value, *others):
    return lax.optimization_barrier((value,) + others)[0]


def spread_tensor(blocks):
    return lax.all_to_all(blocks, "tensor", 0, 0, tiled=True)


def square():
    return lax.axis_size("dp") == 2 and lax.axis_size("context") == 2


def reorder(values):
    if not square():
        return values
    dp, ctx = lax.axis_index("dp"), lax.axis_index("context")
    size = values.shape[-1] // 4
    half = 2 * size
    values = jnp.where(dp == 1, jnp.concatenate([values[..., half:], values[..., :half]], -1), values)
    blocks = [values[..., n * size:(n + 1) * size] for n in range(4)]
    turned = jnp.concatenate([blocks[1], blocks[0], blocks[3], blocks[2]], -1)
    return jnp.where(ctx == 1, turned, values)


def add_bf16(left, right):
    return (left.astype(F32) + right.astype(F32)).astype(BF16)


def tensor_pieces(value):
    count = lax.axis_size("tensor")
    pieces = [value]
    for step in range(1, count):
        pairs = [(n, (n + step) % count) for n in range(count)]
        pieces.append(lax.ppermute(value, "tensor", pairs))
    return pieces


def rows_layout(value):
    return with_layout_constraint(value, Layout(tuple(range(value.ndim))))


def per_device(inputs, cotangent, w_qkv, w_out, w_up, w_down, norm_gains, norm_shifts):
    section = lax.axis_index("section")
    tensors = lax.axis_size("tensor")
    contexts = lax.axis_size("context")
    ctx = lax.axis_index("context")
    micro, _, span, width = inputs.shape
    assert micro == tensors and lax.axis_size("section") == 2 and tensors % 2 == 0
    half_span = span // 2
    count = tensors * span
    own_rows = w_qkv.shape[2]
    share_heads = w_qkv.shape[3] // HEAD_DIM
    half_heads = share_heads * tensors // 2
    heads = -(-half_heads // contexts)
    fast = square() and contexts * 2 == tensors
    first = share_heads - share_heads // 2
    parts = [n for n in (first, share_heads - first) if n] if fast else [1] * heads
    qkv_cols, out_cols, hidden_cols = w_qkv.shape[3] * 3, w_out.shape[1], w_up.shape[2]


    held = {}

    def stage(compute, *jobs):
        made = {name: job() for name, job in jobs}
        leaves, shape = jax.tree.flatten((compute(), made))
        if not leaves:
            return ()
        result, made = jax.tree.unflatten(shape, lax.optimization_barrier(leaves))
        for name, value in made.items():
            held.update(value if isinstance(value, dict) else {name: value})
        return result


    def head_columns(share, each):
        cut, start = [], 0
        for size in parts:
            cut.append(share[:, start:start + size * each])
            start += size * each
        return cut

    def relative_columns(half, each):
        own, far = take(half, ctx), take(half, 1 - ctx)
        cut = []
        for pair in zip(head_columns(own, each), head_columns(far, each)):
            cut.extend(pair)
        return jnp.concatenate(cut, 1)

    def flipped_columns(value, each):
        cut, start = [], 0
        for size in parts:
            middle, end = start + size * each, start + 2 * size * each
            cut += [value[:, middle:end], value[:, start:middle]]
            start = end
        return cut

    def flipped(value):
        edge = 2 * qkv_cols
        return jnp.concatenate(
            flipped_columns(value[:, :edge], 3 * HEAD_DIM)
            + flipped_columns(value[:, edge:], HEAD_DIM), 1)

    def shares_of_columns(value, each):
        own, far, start = [], [], 0
        for size in parts:
            middle, end = start + size * each, start + 2 * size * each
            own.append(value[:, start:middle])
            far.append(value[:, middle:end])
            start = end
        return paired(jnp.concatenate(own, 1)[None], jnp.concatenate(far, 1)[None], ctx, 0)


    qkv_share = w_qkv[0].reshape(3, own_rows, share_heads, HEAD_DIM).transpose(1, 2, 0, 3)
    if fast:
        pieces, place = [], 0
        for size in parts:
            piece = qkv_share[:, place:place + size].transpose(0, 2, 1, 3)
            pieces.append(piece.reshape(own_rows, -1))
            place += size
    else:
        pieces = [qkv_share.reshape(own_rows, -1)]
    attn_share = jnp.concatenate(pieces + [w_out[0].T], 1)

    def over_tensor(share):
        gathered = lax.all_gather(share, "tensor")
        split = gathered.reshape((2, tensors // 2) + share.shape)
        return take(split, section), take(split, 1 - section)

    def joined_columns(value):
        return value.transpose(1, 0, 2).reshape(own_rows, -1)

    def attn_layer(layer):
        kept, came = held["attn_kept"], held["attn_came"]
        half = jnp.where(section == layer, kept, came)
        split = half[:, :, :qkv_cols], half[:, :, qkv_cols:]
        if fast:
            return rows_layout(jnp.concatenate([
                relative_columns(split[0], 3 * HEAD_DIM), relative_columns(split[1], HEAD_DIM)], 1))
        return jnp.concatenate([joined_columns(piece) for piece in split], 1)

    def hidden_layer(name, layer):
        half = jnp.where(section == layer, held[name + "_kept"], held[name + "_came"])
        return rows_layout(joined_columns(half))

    def near_rows(own, flip=False):
        if not square():
            return own
        return swap(flipped(own) if flip else own, "context")

    def far_rows(rows):
        return swap(rows, "dp") if square() else rows

    def all_rows(own, near, own_far, near_far):
        if not square():
            return lax.all_gather(own, ("dp", "context"), axis=0, tiled=True)
        return jnp.concatenate([own, near, own_far, near_far])

    def reduce_dp(partial, block):
        if not square():
            return partial
        rows = partial.shape[0] // 4
        kept = partial[block * rows:(block + 1) * rows]
        return add_bf16(kept, swap(partial[(block + 2) * rows:(block + 3) * rows], "dp"))

    def reduce_ctx(kept, sent, flip=False):
        if not square():
            return lax.psum_scatter(sent, ("dp", "context"), scatter_dimension=0, tiled=True)
        return add_bf16(kept, swap(flipped(sent) if flip else sent, "context"))

    def both_halves(partial):
        return partial + swap(partial.astype(BF16), "section").astype(F32)


    def split_heads(projected, each):
        if fast:
            result, start = [], 0
            for size in parts:
                middle, end = start + size * each, start + 2 * size * each
                result.append([projected[:, start:middle], projected[:, middle:end]])
                start = end
            return result
        shaped = projected.reshape(count, half_heads, -1)
        shaped = jnp.pad(shaped, ((0, 0), (0, contexts * heads - half_heads), (0, 0)))
        shaped = shaped.reshape(count, contexts, heads, -1)
        return [[take(shaped[:, :, n], lax.bitwise_xor(ctx, step), 1) for step in range(contexts)]
                for n in range(heads)]

    def join_heads(parts_list):
        if fast:
            return jnp.concatenate([block for blocks in parts_list for block in blocks], 1)
        shaped = jnp.stack([in_order(blocks, ctx) for blocks in parts_list])
        shaped = shaped.transpose(2, 1, 0, 3).reshape(count, contexts * heads, -1)
        return shaped[:, :half_heads].reshape(count, -1)

    def exchanged(blocks):
        moved = [blocks[0]]
        for step in range(1, contexts):
            pairs = [(n, n ^ step) for n in range(contexts)]
            moved.append(lax.ppermute(blocks[step], "context", pairs))
        return moved

    def to_all_rows(blocks):
        moved = in_order(exchanged(blocks), ctx)
        return moved.reshape(contexts * count, -1)

    def to_own_rows(full):
        shaped = full.reshape(contexts, count, -1)
        return exchanged([take(shaped, lax.bitwise_xor(ctx, step)) for step in range(contexts)])


    norms_share = jnp.concatenate([norm_gains[0], norm_shifts[0]])
    if square():
        norms_near = jnp.concatenate([norms_share, swap(norms_share, "context")], 1)
        norms_own = jnp.concatenate([norms_near, swap(norms_near, "dp")], 1)
    else:
        norms_own = lax.all_gather(norms_share, ("dp", "context"), axis=1, tiled=True)
    norms_other = swap(norms_own, "section")

    def norms_of(layer):
        chosen = jnp.where(section == layer, norms_own, norms_other).astype(F32)
        return chosen[:2], chosen[2:]

    last = len(parts) - 1

    def forward(layer_in, norms, finish_attn, finish_up, finish_down, jobs):
        gains, shifts = norms

        def begin():
            residual = layer_in.astype(F32)
            return residual, normed(residual, gains[0], shifts[0]).astype(BF16)

        residual, normed_a = stage(begin, *jobs[0])
        qkv, out = attn = finish_attn()

        def spread():
            projected = dot(normed_a, qkv, ((1,), (0,))).astype(BF16)
            blocks = split_heads(projected, 3 * HEAD_DIM)
            return [to_all_rows(blocks[0])], blocks[1:]

        packed, blocks = stage(spread, *jobs[1])
        attended, mixed_own = [], []
        for number in range(last + 1):
            if number:
                mixed_own.append(to_own_rows(attended[number - 1][0]))

            def work():
                done = attend(packed[number], parts[number])
                more = [to_all_rows(blocks[number])] if number < last else []
                return done, more
            done, more = stage(work, *(jobs[number + 2] if number < 2 else []))
            attended.append(done)
            packed += more
        if last == 0:
            stage(lambda: (), *jobs[3])
        mixed_own = stage(lambda: mixed_own + [to_own_rows(attended[-1][0])], *jobs[4])
        mixture = join_heads(mixed_own)
        hidden = stage(
            lambda: residual + both_halves(dot(mixture, out, ((1,), (1,)))), *jobs[5])
        normed_b = stage(
            lambda: normed(hidden, gains[1], shifts[1]).astype(BF16), *jobs[6])
        up = finish_up()

        def expand():
            pre_act = dot(normed_b, up, ((1,), (0,)))
            return pre_act, jax.nn.gelu(pre_act).astype(BF16)

        pre_act, activated = stage(expand, *jobs[7])
        down = finish_down()
        layer_out = stage(
            lambda: (hidden + both_halves(dot(activated, down, ((1,), (1,))))).astype(BF16),
            *jobs[8])
        saved = (residual, normed_a, packed, attended, mixture, hidden, normed_b, pre_act)
        return layer_out, saved, attn + (up, down)

    def backward(tag, grad_branch, saved, norms, weights, jobs):
        gains, shifts = norms
        qkv, out, up, down = weights
        residual, normed_a, packed, attended, mixture, hidden, normed_b, pre_act = saved
        grad_in = grad_branch.astype(F32)
        down_name, up_name, attn_name = (tag + name for name in ("down", "up", "attn"))

        def first():
            grad_act = dot(grad_branch, down, ((1,), (0,)))
            activated, gelu_back = jax.vjp(jax.nn.gelu, pre_act)
            grad_pre = gelu_back(grad_act)[0].astype(BF16)
            grad_down = dot(grad_branch, activated.astype(BF16), ((0,), (0,))).astype(BF16)
            return grad_pre, grad_down

        grad_pre, grad_down = stage(first, *jobs[0])

        def second():
            grad_second = both_halves(dot(grad_pre, up, ((1,), (1,))))
            return grad_second, dot(normed_b, grad_pre, ((0,), (0,))).astype(BF16)

        grad_second, grad_up = stage(second, *jobs[1])

        def third():
            _, second_back = jax.vjp(normed, hidden, gains[1], shifts[1])
            grad_hidden_norm, gain_later, shift_later = second_back(grad_second)
            grad_hidden = grad_in + grad_hidden_norm
            grad_attn = grad_hidden.astype(BF16)
            grad_mixture = dot(grad_attn, out, ((1,), (0,))).astype(BF16)
            return grad_hidden, grad_attn, split_heads(grad_mixture, HEAD_DIM), gain_later, shift_later

        late = hold(grad_down, grad_second)
        grad_hidden, grad_attn, blocks, gain_later, shift_later = stage(
            third, (down_name + "1", lambda: reduce_dp(late, 1)), *jobs[2])
        after = hold(grad_down, grad_attn)
        grad_mixed, blocks = stage(
            lambda: ([to_all_rows(blocks[0])], blocks[1:]),
            (down_name + "0", lambda: reduce_dp(after, 0)), *jobs[3])
        grad_packed, returned, grad_out = [], [], None
        held_up = hold(grad_up, grad_mixed[0])

        def reduce_up():
            sent = reduce_dp(held_up, 1)
            return reduce_ctx(reduce_dp(held_up, 0), sent)

        for number in range(last + 1):
            if number:
                returned.append(to_own_rows(grad_packed[number - 1]))

            def work():
                done = attend_back(packed[number], grad_mixed[number], attended[number][0],
                                   attended[number][1], parts[number])
                more = [to_all_rows(blocks[number])] if number < last else []
                extra = grad_out
                if number == 0:
                    extra = dot(grad_attn, mixture, ((0,), (0,))).astype(BF16)
                return done, more, extra
            beside = jobs[5] if number == 1 else []
            if number == 0:
                beside = [
                    (down_name, lambda: reduce_ctx(held[down_name + "0"], held[down_name + "1"])),
                    (up_name, reduce_up)] + list(jobs[4])
            done, more, grad_out = stage(work, *beside)
            grad_packed.append(done)
            grad_mixed += more
        if last == 0:
            stage(lambda: (), *jobs[5])
        returned = stage(lambda: returned + [to_own_rows(grad_packed[-1])], *jobs[6])
        grad_proj = join_heads(returned)

        def fourth():
            grad_first = both_halves(dot(grad_proj, qkv, ((1,), (1,))))
            grad_qkv = dot(normed_a, grad_proj, ((0,), (0,))).astype(BF16)
            return grad_first, jnp.concatenate([grad_qkv, grad_out], 1)

        grad_first, grad_heads = stage(fourth, *jobs[7])

        def fifth():
            _, first_back = jax.vjp(normed, residual, gains[0], shifts[0])
            grad_input_norm, gain_early, shift_early = first_back(grad_first)
            grad_input = (grad_hidden + grad_input_norm).astype(BF16)
            grad_norms = jnp.stack([gain_early, gain_later, shift_early, shift_later])
            return grad_input, grad_norms

        heads_late = hold(grad_heads, grad_first)
        grad_input, grad_norms = stage(
            fifth, (attn_name + "1", lambda: reduce_dp(heads_late, 1)), *jobs[8])
        return grad_input, grad_norms, grad_heads

    def sum_norms(lower, upper):
        chosen = jnp.where(section == 0, lower, upper)
        if not square():
            total = lax.psum(chosen, ("dp", "context", "tensor"))
            place = lax.axis_index("dp") * contexts + ctx
            return lax.dynamic_slice_in_dim(total, place * own_rows, own_rows, 1)
        half = width // 2
        total = chosen[:, :half] + swap(chosen[:, half:], "dp")
        total = total[:, :own_rows] + swap(total[:, own_rows:], "context")
        return functools.reduce(jnp.add, tensor_pieces(total))

    def entry_half(value):
        half = take(value.reshape(micro, 2, half_span, width), section, 1)
        return spread_tensor(reorder(half))

    def entry_rows(mine):
        other = swap(mine, "section")
        return paired(mine[:, None], other[:, None], section, 1).reshape(count, width)

    def exit_rows(value):
        half = take(value.reshape(tensors, 2, half_span, width), section, 1)
        return spread_tensor(reorder(half))

    def place_layers(lower, upper):
        keep = jnp.where(section == 0, lower, upper)
        came = swap(jnp.where(section == 0, upper, lower), "section")
        whole = paired(keep[:, None], came[:, None], section, 1)
        return whole.reshape(1, micro, 1, span, width)

    def own_layer(lower, upper):
        keep = jnp.where(section == 0, lower, upper)
        came = swap(jnp.where(section == 0, upper, lower), "section")
        return paired(keep, came, section, 0)

    def reduce_tensor(blocks):
        return lax.psum_scatter(blocks, "tensor", scatter_dimension=0)

    def hidden_shares(value):
        return value.reshape(own_rows, tensors // 2, hidden_cols).transpose(1, 0, 2)

    def attn_shares(value):
        edge = value.shape[1] * qkv_cols // (qkv_cols + out_cols)
        if fast:
            cut = [shares_of_columns(value[:, :edge], 3 * HEAD_DIM),
                   shares_of_columns(value[:, edge:], HEAD_DIM)]
        else:
            cut = [piece.reshape(own_rows, tensors // 2, -1).transpose(1, 0, 2)
                   for piece in (value[:, :edge], value[:, edge:])]
        return jnp.concatenate(cut, 2)


    attn_both = stage(lambda: over_tensor(attn_share))
    ffn_share = jnp.concatenate([w_up[0], rows_layout(w_down[0].T)], 1)
    norms_zero, norms_one = norms_of(0), norms_of(1)

    def start():
        held["attn_kept"], held["attn_came"] = attn_both[0], swap(attn_both[1], "section")
        own = attn_layer(0)
        near = near_rows(own, True)
        full = all_rows(own, near, far_rows(own), far_rows(near))
        return entry_half(hold(inputs, attn_both)), full

    entry, attn_zero = stage(start)
    entries = entry_rows(entry)
    cut_at = qkv_cols * tensors // 2

    def cut(full):
        return full[:, :cut_at], full[:, cut_at:]

    def ffn_begin():
        half, other = held["ffn"]
        other = swap(other, "section")
        made = {}
        for layer in range(2):
            mine = jnp.where(section == layer, half, other)
            made[f"up{layer}_own"] = rows_layout(joined_columns(mine[:, :, :hidden_cols]))
            made[f"down{layer}_own"] = rows_layout(joined_columns(mine[:, :, hidden_cols:]))
        made["up0_near"] = near_rows(made["up0_own"])
        made["up0_own_far"] = far_rows(made["up0_own"])
        return made

    def near_job(name):
        return (name + "_near", lambda: near_rows(held[name + "_own"], name == "attn1"))

    def far_job(name, which):
        return (f"{name}_{which}_far", lambda: far_rows(held[f"{name}_{which}"]))

    def finish(name):
        return lambda: all_rows(*[held[f"{name}_{end}"]
                                  for end in ("own", "near", "own_far", "near_far")])

    out_zero, saved_zero, weights_zero = forward(
        entries, norms_zero, lambda: cut(attn_zero), finish("up0"), finish("down0"), [
            [],
            [("ffn", lambda: over_tensor(hold(ffn_share, attn_both)))],
            [("begin", ffn_begin)],
            [far_job("up0", "near"), ("attn1_own", lambda: attn_layer(1))],
            [far_job("down0", "own")],
            [],
            [near_job("down0"), far_job("attn1", "own")],
            [far_job("down0", "near"), near_job("attn1")],
            [],
        ])
    out_one, saved_one, weights_one = forward(
        out_zero, norms_one, lambda: cut(finish("attn1")()), finish("up1"), finish("down1"), [
            [far_job("attn1", "near")],
            [far_job("up1", "own")],
            [near_job("up1"), far_job("down1", "own"), ("exit0", lambda: exit_rows(out_zero))],
            [far_job("up1", "near")],
            [("top", lambda: entry_half(hold(cotangent, held["up1_near"])))],
            [],
            [near_job("down1")],
            [far_job("down1", "near")],
            [],
        ])
    top_grad = entry_rows(held["top"])
    grad_one, norm_sum_one, grad_heads_one = backward(
        "one_", top_grad, saved_one, norms_one, weights_one,
        [[], [], [], [], [("exit1", lambda: exit_rows(out_one))], [], [], [], []])
    layer_outputs = place_layers(held["exit0"], held["exit1"])
    grad_zero, norm_sum_zero, grad_heads_zero = backward(
        "zero_", grad_one, saved_zero, norms_zero, weights_zero, [
            [("one_attn0", lambda: reduce_dp(grad_heads_one, 0))],
            [],
            [("one_attn", lambda: reduce_ctx(held["one_attn0"], held["one_attn1"], True))],
            [],
            [("back1", lambda: exit_rows(grad_one))],
            [("down_all", lambda: own_layer(hidden_shares(held["zero_down"]),
                                            hidden_shares(held["one_down"]))),
             ("up_all", lambda: own_layer(hidden_shares(held["zero_up"]),
                                          hidden_shares(held["one_up"])))],
            [],
            [("down_sum", lambda: reduce_tensor(held["down_all"]))],
            [],
        ])

    def finish_up():
        attn_kept = reduce_dp(grad_heads_zero, 0)
        back_zero = exit_rows(grad_zero)
        attn_zero_sum = reduce_ctx(attn_kept, held["zero_attn1"], True)
        attn_all = own_layer(attn_shares(attn_zero_sum), attn_shares(held["one_attn"]))
        return (back_zero, attn_all, reduce_tensor(held["up_all"]),
                sum_norms(norm_sum_zero, norm_sum_one))

    back_zero, attn_all, grad_up, norm_sums = finish_up()
    boundary_grads = place_layers(back_zero, held["back1"])
    attn_total = reduce_tensor(attn_all).astype(F32)
    grad_up = grad_up.astype(F32)
    grad_down = held["down_sum"].astype(F32)
    grad_qkv, grad_out = attn_total[:, :qkv_cols], attn_total[:, qkv_cols:]
    cut_list, place = [], 0
    for size in (parts if fast else [1] * share_heads):
        columns = size * 3 * HEAD_DIM
        cut_list.append(grad_qkv[:, place:place + columns].reshape(own_rows, 3, size, HEAD_DIM))
        place += columns
    grad_qkv = jnp.concatenate(cut_list, 2).transpose(1, 0, 2, 3).reshape(3, own_rows, -1)
    return (
        layer_outputs,
        boundary_grads,
        grad_qkv[None],
        grad_out.T[None],
        grad_up[None],
        grad_down.T[None],
        norm_sums[:2][None],
        norm_sums[2:][None],
    )


def solution(mesh):
    in_specs = (
        P(None, "dp", ("context", "tensor"), None),
        P(None, "dp", ("context", "tensor"), None),
        P("section", None, ("dp", "context"), "tensor"),
        P("section", "tensor", ("dp", "context")),
        P("section", ("dp", "context"), "tensor"),
        P("section", "tensor", ("dp", "context")),
        P("section", None, ("dp", "context")),
        P("section", None, ("dp", "context")),
    )
    out_specs = (
        P("section", None, "dp", ("context", "tensor"), None),
        P("section", None, "dp", ("context", "tensor"), None),
        P("section", None, ("dp", "context"), "tensor"),
        P("section", "tensor", ("dp", "context")),
        P("section", ("dp", "context"), "tensor"),
        P("section", "tensor", ("dp", "context")),
        P("section", None, ("dp", "context")),
        P("section", None, ("dp", "context")),
    )
    return jax.shard_map(
        per_device, mesh=mesh, in_specs=in_specs, out_specs=out_specs, check_vma=False
    )
```

```python
import functools

import jax
import jax.numpy as jnp
from jax import lax
from jax.experimental import pallas as pl
from jax.experimental.pallas import tpu as pltpu
from jax.experimental.layout import Layout, with_layout_constraint
from jax.sharding import PartitionSpec as P

HEAD_DIM = 64
EPS = 1e-05
NEG = -1e30
BLOCK = 512
SCALE = HEAD_DIM ** (-0.5)
F32 = jnp.float32
BF16 = jnp.bfloat16
VMEM_LIMIT = 48 * 1024 * 1024
SEC, DP, CTX, TEN = "section", "dp", "context", "tensor"
ATTN, UP, DOWN, FFN, ENTRY, EXIT, LAST = range(7)
OWN, NEAR, OWN_FAR, NEAR_FAR, KEPT, CAME, SUM_0, SUM_1, SUM, ALL, DONE = range(11)


def centred(values):
    center = values - jnp.mean(values, -1, keepdims=True)
    spread = jnp.mean(center * center, -1, keepdims=True)
    return center, lax.rsqrt(spread + EPS)


def norm_kernel(summed, *refs):
    if summed:
        base_ref, own_ref, far_ref, gain_ref, shift_ref, sum_ref, out_ref = refs
        values = base_ref[...].astype(F32) + own_ref[...] + far_ref[...].astype(F32)
        sum_ref[...] = values
    else:
        base_ref, gain_ref, shift_ref, out_ref = refs
        values = base_ref[...].astype(F32)
    center, scale = centred(values)
    out_ref[...] = (center * scale * gain_ref[...] + shift_ref[...]).astype(BF16)


def norm(base, gain, shift, own=None, far=None):
    count, width = base.shape
    rows = min(256, count)
    wide = pl.BlockSpec((rows, width), lambda i: (i, 0))
    single = pl.BlockSpec((1, width), lambda i: (0, 0))
    summed = own is not None
    values = [base, own, far] if summed else [base]
    shapes = [jax.ShapeDtypeStruct((count, width), BF16)]
    if summed:
        shapes.insert(0, jax.ShapeDtypeStruct((count, width), F32))
    result = pl.pallas_call(
        functools.partial(norm_kernel, summed),
        grid=(count // rows,),
        in_specs=[wide] * len(values) + [single] * 2,
        out_specs=[wide] * len(shapes),
        out_shape=shapes,
        compiler_params=pltpu.CompilerParams(vmem_limit_bytes=VMEM_LIMIT),
        cost_estimate=pl.CostEstimate(
            flops=count * width * 12, bytes_accessed=count * width * 14, transcendentals=count),
        name="norm",
    )(*values, gain[None], shift[None])
    return result if summed else result[0]


def norm_back_kernel(both, value_ref, own_ref, far_ref, base_ref, gain_ref, *outs):
    sums_ref = outs[-1]

    @pl.when(pl.program_id(0) == 0)
    def clear():
        sums_ref[...] = jnp.zeros_like(sums_ref)

    grad = own_ref[...] + far_ref[...].astype(F32)
    center, scale = centred(value_ref[...].astype(F32))
    unit = center * scale
    sums_ref[0:1] += jnp.sum(grad * unit, 0, keepdims=True)
    sums_ref[1:2] += jnp.sum(grad, 0, keepdims=True)
    scaled = grad * gain_ref[...]
    inner = jnp.mean(scaled * unit, -1, keepdims=True)
    total = base_ref[...].astype(F32) + scale * (
        scaled - jnp.mean(scaled, -1, keepdims=True) - unit * inner)
    if both:
        outs[0][...] = total
    outs[-2][...] = total.astype(BF16)


def norm_back(value, own, far, base, gain, both):
    count, width = value.shape
    rows = min(256, count)
    wide = pl.BlockSpec((rows, width), lambda i: (i, 0))
    shapes = [jax.ShapeDtypeStruct((count, width), BF16), jax.ShapeDtypeStruct((2, width), F32)]
    if both:
        shapes.insert(0, jax.ShapeDtypeStruct((count, width), F32))
    return pl.pallas_call(
        functools.partial(norm_back_kernel, both),
        grid=(count // rows,),
        in_specs=[wide] * 4 + [pl.BlockSpec((1, width), lambda i: (0, 0))],
        out_specs=[wide] * (len(shapes) - 1) + [pl.BlockSpec((2, width), lambda i: (0, 0))],
        out_shape=shapes,
        compiler_params=pltpu.CompilerParams(vmem_limit_bytes=VMEM_LIMIT),
        cost_estimate=pl.CostEstimate(
            flops=count * width * 20, bytes_accessed=count * width * 16, transcendentals=count),
        name="norm_back",
    )(value, own, far, base, gain[None])


def dot(left, right, contract):
    return lax.dot_general(left, right, ((contract[0], contract[1]), ((), ())),
                           preferred_element_type=F32)


def attend_kernel(block, heads, rows_ref, all_ref, mix_ref, log_ref):
    place = pl.program_id(0)
    width = heads * HEAD_DIM
    row_ids = lax.broadcasted_iota(jnp.int32, (block, block), 0)
    col_ids = lax.broadcasted_iota(jnp.int32, (block, block), 1)
    for head in range(heads):
        low = head * HEAD_DIM
        queries = rows_ref[:, low:low + HEAD_DIM] * jnp.asarray(SCALE, BF16)

        def step(index, carry, masked):
            top, total, mixed = carry
            span = pl.ds(pl.multiple_of(index * block, block), block)
            keys = all_ref[span, width + low:width + low + HEAD_DIM]
            values = all_ref[span, 2 * width + low:2 * width + low + HEAD_DIM]
            scores = dot(queries, keys, ((1,), (1,)))
            if masked:
                scores = jnp.where(col_ids <= row_ids, scores, NEG)
            new_top = jnp.maximum(top, jnp.max(scores, -1, keepdims=True))
            grown = jnp.exp(scores - new_top)
            shrink = jnp.exp(top - new_top)
            return (
                new_top,
                total * shrink + jnp.sum(grown, -1, keepdims=True),
                mixed * shrink + dot(grown.astype(BF16), values, ((1,), (0,))),
            )

        carry = (
            jnp.full((block, 1), NEG, F32),
            jnp.zeros((block, 1), F32),
            jnp.zeros((block, HEAD_DIM), F32),
        )
        carry = lax.fori_loop(0, place, lambda i, c: step(i, c, False), carry)
        top, total, mixed = step(place, carry, True)
        mix_ref[:, low:low + HEAD_DIM] = (mixed / total).astype(BF16)
        wide = jnp.broadcast_to(top + jnp.log(total), (block, 128))
        log_ref[head] = wide.T[:1]


def attend(packed, heads):
    length, width = packed.shape
    block = min(BLOCK, length)
    return pl.pallas_call(
        functools.partial(attend_kernel, block, heads),
        grid=(length // block,),
        in_specs=[
            pl.BlockSpec((block, width), lambda i: (i, 0)),
            pl.BlockSpec((length, width), lambda i: (0, 0)),
        ],
        out_specs=[
            pl.BlockSpec((block, width // 3), lambda i: (i, 0)),
            pl.BlockSpec((heads, 1, block), lambda i: (0, 0, i)),
        ],
        out_shape=[
            jax.ShapeDtypeStruct((length, width // 3), BF16),
            jax.ShapeDtypeStruct((heads, 1, length), F32),
        ],
        compiler_params=pltpu.CompilerParams(vmem_limit_bytes=VMEM_LIMIT),
        cost_estimate=pl.CostEstimate(
            flops=2 * 2 * length * length * HEAD_DIM * heads,
            bytes_accessed=length * width * 4,
            transcendentals=length * length * heads // 2,
        ),
        name="attend",
    )(packed, packed)


def attend_back_kernel(block, heads, rows_ref, all_ref, grad_ref, mix_ref, log_ref, out_ref,
                       query_sum, inner):
    place = pl.program_id(0)
    count = pl.num_programs(0)
    width = heads * HEAD_DIM
    key_ids = lax.broadcasted_iota(jnp.int32, (block, block), 0)
    query_ids = lax.broadcasted_iota(jnp.int32, (block, block), 1)

    @pl.when(place == 0)
    def prepare():
        query_sum[...] = jnp.zeros_like(query_sum)

        def one(index, carry):
            span = pl.ds(pl.multiple_of(index * block, block), block)
            product = grad_ref[span, :].astype(F32) * mix_ref[span, :].astype(F32)
            for head in range(heads):
                part = product[:, head * HEAD_DIM:(head + 1) * HEAD_DIM]
                inner[head, :, span] = jnp.sum(part.T, 0, keepdims=True)
            return carry

        lax.fori_loop(0, count, one, 0)

    for head in range(heads):
        low = head * HEAD_DIM
        keys = rows_ref[:, width + low:width + low + HEAD_DIM] * jnp.asarray(SCALE, BF16)
        values = rows_ref[:, 2 * width + low:2 * width + low + HEAD_DIM]

        def step(index, carry, masked):
            key_sum, value_sum = carry
            span = pl.ds(pl.multiple_of(index * block, block), block)
            queries = all_ref[span, low:low + HEAD_DIM]
            grads = grad_ref[span, low:low + HEAD_DIM]
            scores = dot(keys, queries, ((1,), (1,)))
            if masked:
                scores = jnp.where(key_ids <= query_ids, scores, NEG)
            probs = jnp.exp(scores - log_ref[head, :, span])
            grad_probs = dot(values, grads, ((1,), (1,)))
            grad_scores = (probs * (grad_probs - inner[head, :, span])).astype(BF16)
            value_sum = value_sum + dot(probs.astype(BF16), grads, ((1,), (0,)))
            key_sum = key_sum + dot(grad_scores, queries, ((1,), (0,)))
            query_sum[head, span, :] += dot(grad_scores, keys, ((0,), (0,)))
            return key_sum, value_sum

        carry = (jnp.zeros((block, HEAD_DIM), F32), jnp.zeros((block, HEAD_DIM), F32))
        carry = step(place, carry, True)
        key_sum, value_sum = lax.fori_loop(
            place + 1, count, lambda i, c: step(i, c, False), carry)
        own = pl.ds(pl.multiple_of(place * block, block), block)
        out_ref[:, low:low + HEAD_DIM] = query_sum[head, own, :].astype(BF16)
        out_ref[:, width + low:width + low + HEAD_DIM] = (key_sum * SCALE).astype(BF16)
        out_ref[:, 2 * width + low:2 * width + low + HEAD_DIM] = value_sum.astype(BF16)


def attend_back(packed, grads, mixture, logs, heads):
    length, width = packed.shape
    block = min(BLOCK, length)
    third = width // 3
    return pl.pallas_call(
        functools.partial(attend_back_kernel, block, heads),
        grid=(length // block,),
        in_specs=[
            pl.BlockSpec((block, width), lambda i: (i, 0)),
            pl.BlockSpec((length, width), lambda i: (0, 0)),
            pl.BlockSpec((length, third), lambda i: (0, 0)),
            pl.BlockSpec((length, third), lambda i: (0, 0)),
            pl.BlockSpec((heads, 1, length), lambda i: (0, 0, 0)),
        ],
        out_specs=pl.BlockSpec((block, width), lambda i: (i, 0)),
        out_shape=jax.ShapeDtypeStruct((length, width), BF16),
        scratch_shapes=[
            pltpu.VMEM((heads, length, HEAD_DIM), F32),
            pltpu.VMEM((heads, 1, length), F32),
        ],
        compiler_params=pltpu.CompilerParams(vmem_limit_bytes=VMEM_LIMIT),
        cost_estimate=pl.CostEstimate(
            flops=2 * 5 * length * length * HEAD_DIM * heads,
            bytes_accessed=length * width * 8,
            transcendentals=length * length * heads // 2,
        ),
        name="attend_back",
    )(packed, packed, grads, mixture, logs)


def swap(value, axis):
    return lax.ppermute(value, axis, [(0, 1), (1, 0)])


def take(buffer, index, axis=0):
    return lax.dynamic_index_in_dim(buffer, index, axis, keepdims=False)


def paired(near, far, place, axis):
    first = jnp.where(place == 0, near, far)
    second = jnp.where(place == 0, far, near)
    return jnp.concatenate([first, second], axis)


def in_order(blocks, place):
    if len(blocks) == 2:
        return paired(blocks[0][None], blocks[1][None], place, 0)
    stacked = jnp.zeros((len(blocks),) + blocks[0].shape, blocks[0].dtype)
    for step, block in enumerate(blocks):
        stacked = lax.dynamic_update_index_in_dim(
            stacked, block, lax.bitwise_xor(place, step), 0)
    return stacked


def hold(value, *others):
    return lax.optimization_barrier((value,) + others)[0]


def spread_tensor(blocks):
    return lax.all_to_all(blocks, TEN, 0, 0, tiled=True)


def square():
    return lax.axis_size(DP) == 2 and lax.axis_size(CTX) == 2


def reorder(values):
    if not square():
        return values
    dp, ctx = lax.axis_index(DP), lax.axis_index(CTX)
    size = values.shape[-1] // 4
    half = 2 * size
    values = jnp.where(dp == 1, jnp.concatenate([values[..., half:], values[..., :half]], -1), values)
    blocks = [values[..., n * size:(n + 1) * size] for n in range(4)]
    turned = jnp.concatenate([blocks[1], blocks[0], blocks[3], blocks[2]], -1)
    return jnp.where(ctx == 1, turned, values)


def add_bf16(left, right):
    return (left.astype(F32) + right.astype(F32)).astype(BF16)


def tensor_pieces(value):
    count = lax.axis_size(TEN)
    pieces = [value]
    for step in range(1, count):
        pairs = [(n, (n + step) % count) for n in range(count)]
        pieces.append(lax.ppermute(value, TEN, pairs))
    return pieces


def rows_layout(value):
    return with_layout_constraint(value, Layout(tuple(range(value.ndim))))


def per_device(inputs, cotangent, w_qkv, w_out, w_up, w_down, norm_gains, norm_shifts):
    section = lax.axis_index(SEC)
    tensors = lax.axis_size(TEN)
    contexts = lax.axis_size(CTX)
    ctx = lax.axis_index(CTX)
    micro, _, span, width = inputs.shape
    assert micro == tensors and lax.axis_size(SEC) == 2 and tensors % 2 == 0
    half_span = span // 2
    count = tensors * span
    own_rows = w_qkv.shape[2]
    share_heads = w_qkv.shape[3] // HEAD_DIM
    half_heads = share_heads * tensors // 2
    heads = -(-half_heads // contexts)
    fast = square() and contexts * 2 == tensors
    first = share_heads - share_heads // 2
    parts = [n for n in (first, share_heads - first) if n] if fast else [1] * heads
    qkv_cols, out_cols, hidden_cols = w_qkv.shape[3] * 3, w_out.shape[1], w_up.shape[2]


    held = {}

    def stage(compute, *jobs):
        made = {}
        for key, job in jobs:
            value = job()
            made.update(value if isinstance(value, dict) else {key: value})
        leaves, shape = jax.tree.flatten((compute(), [*made.values()]))
        if not leaves:
            return ()
        result, new = jax.tree.unflatten(shape, lax.optimization_barrier(leaves))
        held.update(zip(made, new))
        held[LAST] = jax.tree.leaves((result, new))[0]
        return result


    def head_columns(share, each):
        cut, start = [], 0
        for size in parts:
            cut.append(share[:, start:start + size * each])
            start += size * each
        return cut

    def relative_columns(half, each):
        own, far = take(half, ctx), take(half, 1 - ctx)
        cut = []
        for pair in zip(head_columns(own, each), head_columns(far, each)):
            cut.extend(pair)
        return jnp.concatenate(cut, 1)

    def flipped_columns(value, each):
        cut, start = [], 0
        for size in parts:
            middle, end = start + size * each, start + 2 * size * each
            cut += [value[:, middle:end], value[:, start:middle]]
            start = end
        return cut

    def flipped(value):
        edge = 2 * qkv_cols
        return jnp.concatenate(
            flipped_columns(value[:, :edge], 3 * HEAD_DIM)
            + flipped_columns(value[:, edge:], HEAD_DIM), 1)

    def shares_of_columns(value, each):
        own, far, start = [], [], 0
        for size in parts:
            middle, end = start + size * each, start + 2 * size * each
            own.append(value[:, start:middle])
            far.append(value[:, middle:end])
            start = end
        return paired(jnp.concatenate(own, 1)[None], jnp.concatenate(far, 1)[None], ctx, 0)


    qkv_share = w_qkv[0].reshape(3, own_rows, share_heads, HEAD_DIM).transpose(1, 2, 0, 3)
    if fast:
        pieces, place = [], 0
        for size in parts:
            piece = qkv_share[:, place:place + size].transpose(0, 2, 1, 3)
            pieces.append(piece.reshape(own_rows, -1))
            place += size
    else:
        pieces = [qkv_share.reshape(own_rows, -1)]
    attn_share = jnp.concatenate(pieces + [w_out[0].T], 1)

    def over_tensor(share):
        gathered = lax.all_gather(share, TEN)
        split = gathered.reshape((2, tensors // 2) + share.shape)
        return take(split, section), take(split, 1 - section)

    def joined_columns(value):
        return value.transpose(1, 0, 2).reshape(own_rows, -1)

    def attn_layer(layer):
        half = jnp.where(section == layer, held[ATTN, KEPT], held[ATTN, CAME])
        split = half[:, :, :qkv_cols], half[:, :, qkv_cols:]
        if fast:
            return rows_layout(jnp.concatenate([
                relative_columns(split[0], 3 * HEAD_DIM), relative_columns(split[1], HEAD_DIM)], 1))
        return jnp.concatenate([joined_columns(piece) for piece in split], 1)

    def near_rows(own, flip=False):
        if not square():
            return own
        return swap(flipped(own) if flip else own, CTX)

    def far_rows(rows):
        return swap(rows, DP) if square() else rows

    def all_rows(own, near, own_far, near_far):
        if not square():
            return lax.all_gather(own, (DP, CTX), axis=0, tiled=True)
        return jnp.concatenate([own, near, own_far, near_far])

    def reduce_dp(partial, block):
        if not square():
            return partial
        rows = partial.shape[0] // 4
        kept = partial[block * rows:(block + 1) * rows]
        return add_bf16(kept, swap(partial[(block + 2) * rows:(block + 3) * rows], DP))

    def reduce_ctx(kept, sent, flip=False):
        if not square():
            return lax.psum_scatter(sent, (DP, CTX), scatter_dimension=0, tiled=True)
        return add_bf16(kept, swap(flipped(sent) if flip else sent, CTX))

    def both_halves(partial):
        return partial, swap(partial.astype(BF16), SEC)


    def split_heads(projected, each):
        if fast:
            result, start = [], 0
            for size in parts:
                middle, end = start + size * each, start + 2 * size * each
                result.append([projected[:, start:middle], projected[:, middle:end]])
                start = end
            return result
        shaped = projected.reshape(count, half_heads, -1)
        shaped = jnp.pad(shaped, ((0, 0), (0, contexts * heads - half_heads), (0, 0)))
        shaped = shaped.reshape(count, contexts, heads, -1)
        return [[take(shaped[:, :, n], lax.bitwise_xor(ctx, step), 1) for step in range(contexts)]
                for n in range(heads)]

    def join_heads(parts_list):
        if fast:
            joined = [jnp.concatenate(blocks, 1) for blocks in parts_list]
            return jnp.concatenate(lax.optimization_barrier(joined), 1)
        shaped = jnp.stack([in_order(blocks, ctx) for blocks in parts_list])
        shaped = shaped.transpose(2, 1, 0, 3).reshape(count, contexts * heads, -1)
        return shaped[:, :half_heads].reshape(count, -1)

    def exchanged(blocks):
        moved = [blocks[0]]
        for step in range(1, contexts):
            pairs = [(n, n ^ step) for n in range(contexts)]
            moved.append(lax.ppermute(blocks[step], CTX, pairs))
        return moved

    def to_all_rows(blocks):
        moved = in_order(exchanged(blocks), ctx)
        return moved.reshape(contexts * count, -1)

    def to_own_rows(full):
        shaped = full.reshape(contexts, count, -1)
        return exchanged([take(shaped, lax.bitwise_xor(ctx, step)) for step in range(contexts)])


    def gather_norms():
        share = jnp.concatenate([norm_gains[0], norm_shifts[0]])
        if not square():
            own = lax.all_gather(share, (DP, CTX), axis=1, tiled=True)
        else:
            near = jnp.concatenate([share, swap(share, CTX)], 1)
            own = jnp.concatenate([near, swap(near, DP)], 1)
        return own, swap(own, SEC)

    def norms_of(layer):
        chosen = jnp.where(section == layer, *norms).astype(F32)
        return chosen[:2], chosen[2:]

    last = len(parts) - 1

    def forward(layer_in, norms, finish_attn, finish_up, finish_down, jobs):
        gains, shifts = norms

        normed_a = stage(lambda: norm(layer_in, gains[0], shifts[0]), *jobs[0])
        qkv, out = attn = finish_attn()

        def spread():
            projected = dot(normed_a, qkv, ((1,), (0,))).astype(BF16)
            blocks = split_heads(projected, 3 * HEAD_DIM)
            return [to_all_rows(blocks[0])], blocks[1:]

        packed, blocks = stage(spread, *jobs[1])
        attended, mixed_own = [], []
        for number in range(last + 1):
            def work():
                done = attend(packed[number], parts[number])
                more = [to_all_rows(blocks[number])] if number < last else []
                back = [to_own_rows(attended[number - 1][0])] if number else []
                return done, more, back
            done, more, back = stage(work, *(jobs[number + 2] if number < 2 else []))
            attended.append(done)
            packed += more
            mixed_own += back
        if last == 0:
            stage(lambda: (), *jobs[3])
        mixed_own = stage(lambda: mixed_own + [to_own_rows(attended[-1][0])], *jobs[4])
        mixture = join_heads(mixed_own)
        halves = stage(lambda: both_halves(dot(mixture, out, ((1,), (1,)))), *jobs[5])
        hidden, normed_b = stage(
            lambda: norm(layer_in, gains[1], shifts[1], *halves), *jobs[6])
        up = finish_up()

        def expand():
            pre_act = dot(normed_b, up, ((1,), (0,)))
            return pre_act, jax.nn.gelu(pre_act).astype(BF16)

        pre_act, activated = stage(expand, *jobs[7])
        down = finish_down()
        own, far = stage(
            lambda: both_halves(dot(activated, down, ((1,), (1,)))), *jobs[8])
        layer_out = (hidden + own + far.astype(F32)).astype(BF16)
        saved = (layer_in, normed_a, packed, attended, mixture, hidden, normed_b, pre_act, activated)
        return layer_out, saved, attn + (up, down)

    def backward(layer, grad_branch, saved, norms, weights, jobs):
        gains, shifts = norms
        qkv, out, up, down = weights
        layer_in, normed_a, packed, attended, mixture, hidden, normed_b, pre_act, activated = saved

        def first():
            grad_act = dot(grad_branch, down, ((1,), (0,)))
            _, gelu_back = jax.vjp(jax.nn.gelu, pre_act)
            grad_pre = gelu_back(grad_act)[0].astype(BF16)
            grad_down = dot(grad_branch, activated, ((0,), (0,))).astype(BF16)
            return grad_pre, grad_down

        grad_pre, grad_down = stage(first, *jobs[0])

        def second():
            grad_second = both_halves(dot(grad_pre, up, ((1,), (1,))))
            return grad_second, dot(normed_b, grad_pre, ((0,), (0,))).astype(BF16)

        grad_second, grad_up = stage(second, *jobs[1])

        def third():
            grad_hidden, grad_attn, sums = norm_back(
                hidden, *grad_second, grad_branch, gains[1], True)
            grad_mixture = dot(grad_attn, out, ((1,), (0,))).astype(BF16)
            return grad_hidden, grad_attn, split_heads(grad_mixture, HEAD_DIM), sums

        late = hold(grad_down, *grad_second)
        grad_hidden, grad_attn, blocks, later = stage(
            third, ((DOWN, layer, SUM_1), lambda: reduce_dp(late, 1)), *jobs[2])
        after = hold(grad_down, grad_attn)
        grad_mixed, blocks = stage(
            lambda: ([to_all_rows(blocks[0])], blocks[1:]),
            ((DOWN, layer, SUM_0), lambda: reduce_dp(after, 0)), *jobs[3])
        grad_packed, returned, grad_out = [], [], None
        held_up = hold(grad_up, grad_mixed[0])

        def reduce_up():
            sent = reduce_dp(held_up, 1)
            return reduce_ctx(reduce_dp(held_up, 0), sent)


        for number in range(last + 1):
            if number:
                returned.append(to_own_rows(grad_packed[number - 1]))

            def work():
                done = attend_back(packed[number], grad_mixed[number], attended[number][0],
                                   attended[number][1], parts[number])
                more = [to_all_rows(blocks[number])] if number < last else []
                extra = grad_out
                if number == 0:
                    extra = dot(grad_attn, mixture, ((0,), (0,))).astype(BF16)
                return done, more, extra
            beside = jobs[5] if number == 1 else []
            if number == 0:
                beside = [
                    ((DOWN, layer, SUM), lambda: reduce_ctx(
                        held[DOWN, layer, SUM_0], held[DOWN, layer, SUM_1])),
                    ((UP, layer, SUM), reduce_up)] + list(jobs[4])
            done, more, grad_out = stage(work, *beside)
            grad_packed.append(done)
            grad_mixed += more
        if last == 0:
            stage(lambda: (), *jobs[5])
        returned = stage(lambda: returned + [to_own_rows(grad_packed[-1])], *jobs[6])
        grad_proj = join_heads(returned)

        def fourth():
            grad_first = both_halves(dot(grad_proj, qkv, ((1,), (1,))))
            grad_qkv = dot(normed_a, grad_proj, ((0,), (0,))).astype(BF16)
            return grad_first, jnp.concatenate([grad_qkv, grad_out], 1)

        grad_first, grad_heads = stage(fourth, *jobs[7])

        def fifth():
            grad_input, early = norm_back(
                layer_in, *grad_first, grad_hidden, gains[0], False)
            return grad_input, jnp.stack([early[0], later[0], early[1], later[1]])

        heads_late = hold(grad_heads, *grad_first)
        grad_input, grad_norms = stage(
            fifth, ((ATTN, layer, SUM_1), lambda: reduce_dp(heads_late, 1)), *jobs[8])
        return grad_input, grad_norms, grad_heads

    def sum_norms(lower, upper):
        chosen = jnp.where(section == 0, lower, upper)
        if not square():
            total = lax.psum(chosen, (DP, CTX, TEN))
            place = lax.axis_index(DP) * contexts + ctx
            return lax.dynamic_slice_in_dim(total, place * own_rows, own_rows, 1)
        half = width // 2
        total = chosen[:, :half] + swap(chosen[:, half:], DP)
        total = total[:, :own_rows] + swap(total[:, own_rows:], CTX)
        return functools.reduce(jnp.add, tensor_pieces(total))

    def entry_half(value):
        half = take(value.reshape(micro, 2, half_span, width), section, 1)
        return spread_tensor(reorder(half))

    def entry_rows(mine):
        other = swap(mine, SEC)
        return paired(mine[:, None], other[:, None], section, 1).reshape(count, width)

    def exit_rows(value):
        half = take(value.reshape(tensors, 2, half_span, width), section, 1)
        return spread_tensor(reorder(half))

    def place_layers(lower, upper):
        keep = jnp.where(section == 0, lower, upper)
        came = swap(jnp.where(section == 0, upper, lower), SEC)
        whole = paired(keep[:, None], came[:, None], section, 1)
        return whole.reshape(1, micro, 1, span, width)

    def own_layer(lower, upper):
        keep = jnp.where(section == 0, lower, upper)
        came = swap(jnp.where(section == 0, upper, lower), SEC)
        return paired(keep, came, section, 0)

    def reduce_tensor(blocks):
        return lax.psum_scatter(blocks, TEN, scatter_dimension=0)

    def reduce_direct(blocks):
        count, place = tensors, lax.axis_index(TEN)
        total = take(blocks, place).astype(F32)
        for step in range(1, count):
            pairs = [(n, (n + step) % count) for n in range(count)]
            sent = take(blocks, lax.rem(place + step, count))
            total = total + lax.ppermute(sent, TEN, pairs).astype(F32)
        return total

    def hidden_shares(value):
        return value.reshape(own_rows, tensors // 2, hidden_cols).transpose(1, 0, 2)

    def attn_shares(value):
        edge = value.shape[1] * qkv_cols // (qkv_cols + out_cols)
        if fast:
            cut = [shares_of_columns(value[:, :edge], 3 * HEAD_DIM),
                   shares_of_columns(value[:, edge:], HEAD_DIM)]
        else:
            cut = [piece.reshape(own_rows, tensors // 2, -1).transpose(1, 0, 2)
                   for piece in (value[:, :edge], value[:, edge:])]
        return jnp.concatenate(cut, 2)


    attn_both, entry, norms = stage(
        lambda: (over_tensor(attn_share), entry_half(inputs), gather_norms()))
    ffn_share = jnp.concatenate([w_up[0], rows_layout(w_down[0].T)], 1)
    norms_zero, norms_one = norms_of(0), norms_of(1)

    def start():
        held[ATTN, KEPT], held[ATTN, CAME] = attn_both[0], swap(attn_both[1], SEC)
        own = attn_layer(0)
        near = near_rows(own, True)
        full = all_rows(own, near, far_rows(own), far_rows(near))
        return entry_rows(entry), full, norms_zero, norms_one

    entries, attn_zero, norms_zero, norms_one = stage(start)
    cut_at = qkv_cols * tensors // 2

    def cut(full):
        return full[:, :cut_at], full[:, cut_at:]

    def ffn_begin():
        half, other = over_tensor(ffn_share)
        other = swap(other, SEC)
        made = {}
        for layer in range(2):
            mine = jnp.where(section == layer, half, other)
            made[UP, layer, OWN] = rows_layout(joined_columns(mine[:, :, :hidden_cols]))
            made[DOWN, layer, OWN] = rows_layout(joined_columns(mine[:, :, hidden_cols:]))
        return made

    def late(value):
        return hold(value, held[LAST])

    def near_job(what, layer):
        return (what, layer, NEAR), lambda: near_rows(late(held[what, layer, OWN]), what == ATTN)

    def far_job(what, layer, state, start=late):
        return ((what, layer, OWN_FAR if state == OWN else NEAR_FAR),
                lambda: far_rows(start(held[what, layer, state])))

    def finish(what, layer):
        return lambda: all_rows(*[held.pop((what, layer, state))
                                  for state in (OWN, NEAR, OWN_FAR, NEAR_FAR)])

    out_zero, saved_zero, weights_zero = forward(
        entries, norms_zero, lambda: cut(attn_zero), finish(UP, 0), finish(DOWN, 0), [
            [],
            [(FFN, ffn_begin)],
            [near_job(UP, 0), far_job(UP, 0, OWN)],
            [far_job(UP, 0, NEAR), ((ATTN, 1, OWN), lambda: attn_layer(1))],
            [far_job(DOWN, 0, OWN)],
            [],
            [near_job(DOWN, 0), far_job(ATTN, 1, OWN)],
            [far_job(DOWN, 0, NEAR), near_job(ATTN, 1)],
            [],
        ])
    held[EXIT, 0, OWN] = out_zero
    out_one, saved_one, weights_one = forward(
        out_zero, norms_one, lambda: cut(finish(ATTN, 1)()), finish(UP, 1), finish(DOWN, 1), [
            [far_job(ATTN, 1, NEAR, lambda value: value)],
            [far_job(UP, 1, OWN)],
            [near_job(UP, 1), far_job(DOWN, 1, OWN),
             ((EXIT, 0), lambda: exit_rows(late(held.pop((EXIT, 0, OWN)))))],
            [far_job(UP, 1, NEAR)],
            [((ENTRY, 1), lambda: entry_half(hold(cotangent, held[UP, 1, NEAR_FAR])))],
            [],
            [near_job(DOWN, 1)],
            [far_job(DOWN, 1, NEAR)],
            [],
        ])
    top_grad = entry_rows(held.pop((ENTRY, 1)))
    held[EXIT, 1, OWN] = out_one
    grad_one, norm_sum_one, grad_heads_one = backward(
        1, top_grad, saved_one, norms_one, weights_one, [
            [], [], [], [], [((EXIT, 1), lambda: exit_rows(held.pop((EXIT, 1, OWN))))],
            [], [], [], []])
    held[EXIT, 0, OWN] = grad_one

    def all_shares(what):
        return (what, ALL), lambda: own_layer(hidden_shares(held.pop((what, 0, SUM))),
                                              hidden_shares(held.pop((what, 1, SUM))))

    def sum_shares(what):
        return (what, DONE), lambda: reduce_tensor(held.pop((what, ALL)))

    grad_zero, norm_sum_zero, grad_heads_zero = backward(
        0, grad_one, saved_zero, norms_zero, weights_zero, [
            [((ATTN, 1, SUM_0), lambda: reduce_dp(grad_heads_one, 0))],
            [],
            [((ATTN, 1, SUM), lambda: reduce_ctx(
                held[ATTN, 1, SUM_0], held[ATTN, 1, SUM_1], True))],
            [],
            [((EXIT, 2), lambda: exit_rows(held.pop((EXIT, 0, OWN))))],
            [],
            [all_shares(DOWN), all_shares(UP)],
            [],
            [sum_shares(DOWN)],
        ])

    def last_rows():
        sent = held[ATTN, 0, SUM_1]
        return reduce_ctx(reduce_dp(grad_heads_zero, 0), sent, True), exit_rows(grad_zero)

    attn_zero_sum, back_zero = stage(last_rows, sum_shares(UP))
    attn_all = own_layer(attn_shares(attn_zero_sum), attn_shares(held[ATTN, 1, SUM]))
    attn_total = reduce_direct(attn_all)
    layer_outputs = place_layers(held[EXIT, 0], held[EXIT, 1])
    boundary_grads = place_layers(back_zero, held[EXIT, 2])
    grad_down, grad_up = held[DOWN, DONE].astype(F32).T, held[UP, DONE].astype(F32)
    norm_sums = sum_norms(hold(norm_sum_zero, attn_all), norm_sum_one)
    grad_qkv, grad_out = attn_total[:, :qkv_cols], attn_total[:, qkv_cols:]
    cut_list, place = [], 0
    for size in (parts if fast else [1] * share_heads):
        columns = size * 3 * HEAD_DIM
        cut_list.append(grad_qkv[:, place:place + columns].reshape(own_rows, 3, size, HEAD_DIM))
        place += columns
    grad_qkv = jnp.concatenate(cut_list, 2).transpose(1, 0, 2, 3).reshape(3, own_rows, -1)
    return (
        layer_outputs,
        boundary_grads,
        grad_qkv[None],
        grad_out.T[None],
        grad_up[None],
        grad_down[None],
        norm_sums[:2][None],
        norm_sums[2:][None],
    )


def solution(mesh):
    in_specs = (
        P(None, DP, (CTX, TEN), None),
        P(None, DP, (CTX, TEN), None),
        P(SEC, None, (DP, CTX), TEN),
        P(SEC, TEN, (DP, CTX)),
        P(SEC, (DP, CTX), TEN),
        P(SEC, TEN, (DP, CTX)),
        P(SEC, None, (DP, CTX)),
        P(SEC, None, (DP, CTX)),
    )
    out_specs = (
        P(SEC, None, DP, (CTX, TEN), None),
        P(SEC, None, DP, (CTX, TEN), None),
        P(SEC, None, (DP, CTX), TEN),
        P(SEC, TEN, (DP, CTX)),
        P(SEC, (DP, CTX), TEN),
        P(SEC, TEN, (DP, CTX)),
        P(SEC, None, (DP, CTX)),
        P(SEC, None, (DP, CTX)),
    )
    return jax.shard_map(
        per_device, mesh=mesh, in_specs=in_specs, out_specs=out_specs, check_vma=False
    )
```

```python
import functools

import jax
import jax.numpy as jnp
from jax import lax
from jax.experimental import pallas as pl
from jax.experimental.pallas import tpu as pltpu
from jax.experimental.layout import Layout, with_layout_constraint
from jax.sharding import PartitionSpec as P

HEAD_DIM = 64
EPS = 1e-05
NEG = -1e30
BLOCK = 1024
SCALE = HEAD_DIM ** (-0.5)
F32 = jnp.float32
BF16 = jnp.bfloat16
VMEM_LIMIT = 48 * 1024 * 1024
SEC, DP, CTX, TEN = "section", "dp", "context", "tensor"
ATTN, UP, DOWN, FFN, ENTRY, EXIT, LAST = range(7)
OWN, NEAR, OWN_FAR, NEAR_FAR, KEPT, CAME, SUM_0, SUM_1, SUM, ALL, DONE = range(11)


def centred(values):
    center = values - jnp.mean(values, -1, keepdims=True)
    spread = jnp.mean(center * center, -1, keepdims=True)
    return center, lax.rsqrt(spread + EPS)


def norm_kernel(summed, *refs):
    if summed:
        base_ref, own_ref, far_ref, gain_ref, shift_ref, sum_ref, out_ref = refs
        values = base_ref[...].astype(F32) + own_ref[...] + far_ref[...].astype(F32)
        sum_ref[...] = values
    else:
        base_ref, gain_ref, shift_ref, out_ref = refs
        values = base_ref[...].astype(F32)
    center, scale = centred(values)
    out_ref[...] = (center * scale * gain_ref[...] + shift_ref[...]).astype(BF16)


def norm(base, gain, shift, own=None, far=None):
    count, width = base.shape
    rows = min(256, count)
    wide = pl.BlockSpec((rows, width), lambda i: (i, 0))
    single = pl.BlockSpec((1, width), lambda i: (0, 0))
    summed = own is not None
    values = [base, own, far] if summed else [base]
    shapes = [jax.ShapeDtypeStruct((count, width), BF16)]
    if summed:
        shapes.insert(0, jax.ShapeDtypeStruct((count, width), F32))
    result = pl.pallas_call(
        functools.partial(norm_kernel, summed),
        grid=(count // rows,),
        in_specs=[wide] * len(values) + [single] * 2,
        out_specs=[wide] * len(shapes),
        out_shape=shapes,
        compiler_params=pltpu.CompilerParams(vmem_limit_bytes=VMEM_LIMIT),
        cost_estimate=pl.CostEstimate(
            flops=count * width * 12, bytes_accessed=count * width * 14, transcendentals=count),
        name="norm",
    )(*values, gain[None], shift[None])
    return result if summed else result[0]


def norm_back_kernel(both, value_ref, own_ref, far_ref, base_ref, gain_ref, *outs):
    sums_ref = outs[-1]

    @pl.when(pl.program_id(0) == 0)
    def clear():
        sums_ref[...] = jnp.zeros_like(sums_ref)

    grad = own_ref[...] + far_ref[...].astype(F32)
    center, scale = centred(value_ref[...].astype(F32))
    unit = center * scale
    sums_ref[0:1] += jnp.sum(grad * unit, 0, keepdims=True)
    sums_ref[1:2] += jnp.sum(grad, 0, keepdims=True)
    scaled = grad * gain_ref[...]
    inner = jnp.mean(scaled * unit, -1, keepdims=True)
    total = base_ref[...].astype(F32) + scale * (
        scaled - jnp.mean(scaled, -1, keepdims=True) - unit * inner)
    if both:
        outs[0][...] = total
    outs[-2][...] = total.astype(BF16)


def norm_back(value, own, far, base, gain, both):
    count, width = value.shape
    rows = min(256, count)
    wide = pl.BlockSpec((rows, width), lambda i: (i, 0))
    shapes = [jax.ShapeDtypeStruct((count, width), BF16), jax.ShapeDtypeStruct((2, width), F32)]
    if both:
        shapes.insert(0, jax.ShapeDtypeStruct((count, width), F32))
    return pl.pallas_call(
        functools.partial(norm_back_kernel, both),
        grid=(count // rows,),
        in_specs=[wide] * 4 + [pl.BlockSpec((1, width), lambda i: (0, 0))],
        out_specs=[wide] * (len(shapes) - 1) + [pl.BlockSpec((2, width), lambda i: (0, 0))],
        out_shape=shapes,
        compiler_params=pltpu.CompilerParams(vmem_limit_bytes=VMEM_LIMIT),
        cost_estimate=pl.CostEstimate(
            flops=count * width * 20, bytes_accessed=count * width * 16, transcendentals=count),
        name="norm_back",
    )(value, own, far, base, gain[None])


def dot(left, right, contract):
    return lax.dot_general(left, right, ((contract[0], contract[1]), ((), ())),
                           preferred_element_type=F32)


def attend_kernel(block, heads, rows_ref, all_ref, mix_ref, log_ref):
    place = pl.program_id(0)
    width = heads * HEAD_DIM
    row_ids = lax.broadcasted_iota(jnp.int32, (block, block), 0)
    col_ids = lax.broadcasted_iota(jnp.int32, (block, block), 1)
    for head in range(heads):
        low = head * HEAD_DIM
        queries = rows_ref[:, low:low + HEAD_DIM] * jnp.asarray(SCALE, BF16)

        def step(index, carry, masked):
            top, total, mixed = carry
            span = pl.ds(pl.multiple_of(index * block, block), block)
            keys = all_ref[span, width + low:width + low + HEAD_DIM]
            values = all_ref[span, 2 * width + low:2 * width + low + HEAD_DIM]
            scores = dot(queries, keys, ((1,), (1,)))
            if masked:
                scores = jnp.where(col_ids <= row_ids, scores, NEG)
            new_top = jnp.maximum(top, jnp.max(scores, -1, keepdims=True))
            grown = jnp.exp(scores - new_top)
            shrink = jnp.exp(top - new_top)
            return (
                new_top,
                total * shrink + jnp.sum(grown, -1, keepdims=True),
                mixed * shrink + dot(grown.astype(BF16), values, ((1,), (0,))),
            )

        carry = (
            jnp.full((block, 1), NEG, F32),
            jnp.zeros((block, 1), F32),
            jnp.zeros((block, HEAD_DIM), F32),
        )
        carry = lax.fori_loop(0, place, lambda i, c: step(i, c, False), carry)
        top, total, mixed = step(place, carry, True)
        mix_ref[:, low:low + HEAD_DIM] = (mixed / total).astype(BF16)
        wide = jnp.broadcast_to(top + jnp.log(total), (block, 128))
        log_ref[head] = wide.T[:1]


def attend(packed, heads):
    length, width = packed.shape
    block = min(BLOCK, length)
    return pl.pallas_call(
        functools.partial(attend_kernel, block, heads),
        grid=(length // block,),
        in_specs=[
            pl.BlockSpec((block, width), lambda i: (i, 0)),
            pl.BlockSpec((length, width), lambda i: (0, 0)),
        ],
        out_specs=[
            pl.BlockSpec((block, width // 3), lambda i: (i, 0)),
            pl.BlockSpec((heads, 1, block), lambda i: (0, 0, i)),
        ],
        out_shape=[
            jax.ShapeDtypeStruct((length, width // 3), BF16),
            jax.ShapeDtypeStruct((heads, 1, length), F32),
        ],
        compiler_params=pltpu.CompilerParams(vmem_limit_bytes=VMEM_LIMIT),
        cost_estimate=pl.CostEstimate(
            flops=2 * 2 * length * length * HEAD_DIM * heads,
            bytes_accessed=length * width * 4,
            transcendentals=length * length * heads // 2,
        ),
        name="attend",
    )(packed, packed)


def attend_back_kernel(block, heads, rows_ref, all_ref, grad_ref, mix_ref, log_ref, out_ref,
                       query_sum, inner):
    place = pl.program_id(0)
    count = pl.num_programs(0)
    width = heads * HEAD_DIM
    key_ids = lax.broadcasted_iota(jnp.int32, (block, block), 0)
    query_ids = lax.broadcasted_iota(jnp.int32, (block, block), 1)

    @pl.when(place == 0)
    def prepare():
        query_sum[...] = jnp.zeros_like(query_sum)

        def one(index, carry):
            span = pl.ds(pl.multiple_of(index * block, block), block)
            product = grad_ref[span, :].astype(F32) * mix_ref[span, :].astype(F32)
            for head in range(heads):
                part = product[:, head * HEAD_DIM:(head + 1) * HEAD_DIM]
                inner[head, :, span] = jnp.sum(part.T, 0, keepdims=True)
            return carry

        lax.fori_loop(0, count, one, 0)

    for head in range(heads):
        low = head * HEAD_DIM
        keys = rows_ref[:, width + low:width + low + HEAD_DIM] * jnp.asarray(SCALE, BF16)
        values = rows_ref[:, 2 * width + low:2 * width + low + HEAD_DIM]

        def step(index, carry, masked):
            key_sum, value_sum = carry
            span = pl.ds(pl.multiple_of(index * block, block), block)
            queries = all_ref[span, low:low + HEAD_DIM]
            grads = grad_ref[span, low:low + HEAD_DIM]
            scores = dot(keys, queries, ((1,), (1,)))
            if masked:
                scores = jnp.where(key_ids <= query_ids, scores, NEG)
            probs = jnp.exp(scores - log_ref[head, :, span])
            grad_probs = dot(values, grads, ((1,), (1,)))
            grad_scores = (probs * (grad_probs - inner[head, :, span])).astype(BF16)
            value_sum = value_sum + dot(probs.astype(BF16), grads, ((1,), (0,)))
            key_sum = key_sum + dot(grad_scores, queries, ((1,), (0,)))
            query_sum[head, span, :] += dot(grad_scores, keys, ((0,), (0,)))
            return key_sum, value_sum

        carry = (jnp.zeros((block, HEAD_DIM), F32), jnp.zeros((block, HEAD_DIM), F32))
        carry = step(place, carry, True)
        key_sum, value_sum = lax.fori_loop(
            place + 1, count, lambda i, c: step(i, c, False), carry)
        own = pl.ds(pl.multiple_of(place * block, block), block)
        out_ref[:, low:low + HEAD_DIM] = query_sum[head, own, :].astype(BF16)
        out_ref[:, width + low:width + low + HEAD_DIM] = (key_sum * SCALE).astype(BF16)
        out_ref[:, 2 * width + low:2 * width + low + HEAD_DIM] = value_sum.astype(BF16)


def attend_back(packed, grads, mixture, logs, heads):
    length, width = packed.shape
    block = min(BLOCK, length)
    third = width // 3
    return pl.pallas_call(
        functools.partial(attend_back_kernel, block, heads),
        grid=(length // block,),
        in_specs=[
            pl.BlockSpec((block, width), lambda i: (i, 0)),
            pl.BlockSpec((length, width), lambda i: (0, 0)),
            pl.BlockSpec((length, third), lambda i: (0, 0)),
            pl.BlockSpec((length, third), lambda i: (0, 0)),
            pl.BlockSpec((heads, 1, length), lambda i: (0, 0, 0)),
        ],
        out_specs=pl.BlockSpec((block, width), lambda i: (i, 0)),
        out_shape=jax.ShapeDtypeStruct((length, width), BF16),
        scratch_shapes=[
            pltpu.VMEM((heads, length, HEAD_DIM), F32),
            pltpu.VMEM((heads, 1, length), F32),
        ],
        compiler_params=pltpu.CompilerParams(vmem_limit_bytes=VMEM_LIMIT),
        cost_estimate=pl.CostEstimate(
            flops=2 * 5 * length * length * HEAD_DIM * heads,
            bytes_accessed=length * width * 8,
            transcendentals=length * length * heads // 2,
        ),
        name="attend_back",
    )(packed, packed, grads, mixture, logs)


def swap(value, axis):
    return lax.ppermute(value, axis, [(0, 1), (1, 0)])


def take(buffer, index, axis=0):
    return lax.dynamic_index_in_dim(buffer, index, axis, keepdims=False)


def paired(near, far, place, axis):
    first = jnp.where(place == 0, near, far)
    second = jnp.where(place == 0, far, near)
    return jnp.concatenate([first, second], axis)


def in_order(blocks, place):
    if len(blocks) == 2:
        return paired(blocks[0][None], blocks[1][None], place, 0)
    stacked = jnp.zeros((len(blocks),) + blocks[0].shape, blocks[0].dtype)
    for step, block in enumerate(blocks):
        stacked = lax.dynamic_update_index_in_dim(
            stacked, block, lax.bitwise_xor(place, step), 0)
    return stacked


def hold(value, *others):
    return lax.optimization_barrier((value,) + others)[0]


def spread_tensor(blocks):
    return lax.all_to_all(blocks, TEN, 0, 0, tiled=True)


def square():
    return lax.axis_size(DP) == 2 and lax.axis_size(CTX) == 2


def reorder(values):
    if not square():
        return values
    dp, ctx = lax.axis_index(DP), lax.axis_index(CTX)
    size = values.shape[-1] // 4
    half = 2 * size
    values = jnp.where(dp == 1, jnp.concatenate([values[..., half:], values[..., :half]], -1), values)
    blocks = [values[..., n * size:(n + 1) * size] for n in range(4)]
    turned = jnp.concatenate([blocks[1], blocks[0], blocks[3], blocks[2]], -1)
    return jnp.where(ctx == 1, turned, values)


def add_bf16(left, right):
    return (left.astype(F32) + right.astype(F32)).astype(BF16)


def tensor_pieces(value):
    count = lax.axis_size(TEN)
    pieces = [value]
    for step in range(1, count):
        pairs = [(n, (n + step) % count) for n in range(count)]
        pieces.append(lax.ppermute(value, TEN, pairs))
    return pieces


def rows_layout(value):
    return with_layout_constraint(value, Layout(tuple(range(value.ndim))))


def per_device(inputs, cotangent, w_qkv, w_out, w_up, w_down, norm_gains, norm_shifts):
    section = lax.axis_index(SEC)
    tensors = lax.axis_size(TEN)
    contexts = lax.axis_size(CTX)
    ctx = lax.axis_index(CTX)
    micro, _, span, width = inputs.shape
    assert micro == tensors and lax.axis_size(SEC) == 2 and tensors % 2 == 0
    half_span = span // 2
    count = tensors * span
    own_rows = w_qkv.shape[2]
    share_heads = w_qkv.shape[3] // HEAD_DIM
    half_heads = share_heads * tensors // 2
    heads = -(-half_heads // contexts)
    fast = square() and contexts * 2 == tensors
    first = share_heads - share_heads // 2
    parts = [n for n in (first, share_heads - first) if n] if fast else [1] * heads
    qkv_cols, out_cols, hidden_cols = w_qkv.shape[3] * 3, w_out.shape[1], w_up.shape[2]


    held = {}

    def stage(compute, *jobs):
        made = {}
        for key, job in jobs:
            value = held[key] if job is None else job()
            made.update(value if isinstance(value, dict) else {key: value})
        leaves, shape = jax.tree.flatten((compute(), [*made.values()]))
        if not leaves:
            return ()
        result, new = jax.tree.unflatten(shape, lax.optimization_barrier(leaves))
        held.update(zip(made, new))
        held[LAST] = jax.tree.leaves((result, new))[0]
        return result


    def head_columns(share, each):
        cut, start = [], 0
        for size in parts:
            cut.append(share[:, start:start + size * each])
            start += size * each
        return cut

    def relative_columns(half, each):
        own, far = take(half, ctx), take(half, 1 - ctx)
        cut = []
        for pair in zip(head_columns(own, each), head_columns(far, each)):
            cut.extend(pair)
        return jnp.concatenate(cut, 1)

    def flipped_columns(value, each):
        cut, start = [], 0
        for size in parts:
            middle, end = start + size * each, start + 2 * size * each
            cut += [value[:, middle:end], value[:, start:middle]]
            start = end
        return cut

    def flipped(value):
        edge = 2 * qkv_cols
        return jnp.concatenate(
            flipped_columns(value[:, :edge], 3 * HEAD_DIM)
            + flipped_columns(value[:, edge:], HEAD_DIM), 1)

    def shares_of_columns(value, each):
        own, far, start = [], [], 0
        for size in parts:
            middle, end = start + size * each, start + 2 * size * each
            own.append(value[:, start:middle])
            far.append(value[:, middle:end])
            start = end
        return paired(jnp.concatenate(own, 1)[None], jnp.concatenate(far, 1)[None], ctx, 0)


    qkv_share = w_qkv[0].reshape(3, own_rows, share_heads, HEAD_DIM).transpose(1, 2, 0, 3)
    if fast:
        pieces, place = [], 0
        for size in parts:
            piece = qkv_share[:, place:place + size].transpose(0, 2, 1, 3)
            pieces.append(piece.reshape(own_rows, -1))
            place += size
    else:
        pieces = [qkv_share.reshape(own_rows, -1)]
    attn_share = jnp.concatenate(pieces + [w_out[0].T], 1)

    def over_tensor(share):
        gathered = lax.all_gather(share, TEN)
        split = gathered.reshape((2, tensors // 2) + share.shape)
        return take(split, section), take(split, 1 - section)

    def joined_columns(value):
        return value.transpose(1, 0, 2).reshape(own_rows, -1)

    def attn_layer(layer):
        half = jnp.where(section == layer, held[ATTN, KEPT], held[ATTN, CAME])
        split = half[:, :, :qkv_cols], half[:, :, qkv_cols:]
        if fast:
            return rows_layout(jnp.concatenate([
                relative_columns(split[0], 3 * HEAD_DIM), relative_columns(split[1], HEAD_DIM)], 1))
        return jnp.concatenate([joined_columns(piece) for piece in split], 1)

    def near_rows(own, flip=False):
        if not square():
            return own
        return swap(flipped(own) if flip else own, CTX)

    def far_rows(rows):
        return swap(rows, DP) if square() else rows

    def all_rows(own, near, own_far, near_far):
        if not square():
            return lax.all_gather(own, (DP, CTX), axis=0, tiled=True)
        return jnp.concatenate([own, near, own_far, near_far])

    def reduce_dp(partial, block):
        if not square():
            return partial
        rows = partial.shape[0] // 4
        kept = partial[block * rows:(block + 1) * rows]
        return add_bf16(kept, swap(partial[(block + 2) * rows:(block + 3) * rows], DP))

    def reduce_ctx(kept, sent, flip=False):
        if not square():
            return lax.psum_scatter(sent, (DP, CTX), scatter_dimension=0, tiled=True)
        return add_bf16(kept, swap(flipped(sent) if flip else sent, CTX))

    def both_halves(partial):
        return partial, swap(partial.astype(BF16), SEC)


    def split_heads(projected, each):
        if fast:
            result, start = [], 0
            for size in parts:
                middle, end = start + size * each, start + 2 * size * each
                result.append([projected[:, start:middle], projected[:, middle:end]])
                start = end
            return result
        shaped = projected.reshape(count, half_heads, -1)
        shaped = jnp.pad(shaped, ((0, 0), (0, contexts * heads - half_heads), (0, 0)))
        shaped = shaped.reshape(count, contexts, heads, -1)
        return [[take(shaped[:, :, n], lax.bitwise_xor(ctx, step), 1) for step in range(contexts)]
                for n in range(heads)]

    def join_heads(parts_list):
        if fast:
            joined = [jnp.concatenate(blocks, 1) for blocks in parts_list]
            return jnp.concatenate(lax.optimization_barrier(joined), 1)
        shaped = jnp.stack([in_order(blocks, ctx) for blocks in parts_list])
        shaped = shaped.transpose(2, 1, 0, 3).reshape(count, contexts * heads, -1)
        return shaped[:, :half_heads].reshape(count, -1)

    def exchanged(blocks):
        moved = [blocks[0]]
        for step in range(1, contexts):
            pairs = [(n, n ^ step) for n in range(contexts)]
            moved.append(lax.ppermute(blocks[step], CTX, pairs))
        return moved

    def to_all_rows(blocks):
        moved = in_order(exchanged(blocks), ctx)
        return moved.reshape(contexts * count, -1)

    def to_own_rows(full):
        shaped = full.reshape(contexts, count, -1)
        return exchanged([take(shaped, lax.bitwise_xor(ctx, step)) for step in range(contexts)])


    def gather_norms():
        share = jnp.concatenate([norm_gains[0], norm_shifts[0]])
        if not square():
            own = lax.all_gather(share, (DP, CTX), axis=1, tiled=True)
        else:
            near = jnp.concatenate([share, swap(share, CTX)], 1)
            own = jnp.concatenate([near, swap(near, DP)], 1)
        return own, swap(own, SEC)

    def norms_of(layer):
        chosen = jnp.where(section == layer, *norms).astype(F32)
        return chosen[:2], chosen[2:]

    last = len(parts) - 1

    def forward(layer_in, norms, finish_attn, finish_up, finish_down, jobs):
        gains, shifts = norms

        normed_a = stage(lambda: norm(layer_in, gains[0], shifts[0]), *jobs[0])
        qkv, out = attn = finish_attn()

        def spread():
            projected = dot(normed_a, qkv, ((1,), (0,))).astype(BF16)
            blocks = split_heads(projected, 3 * HEAD_DIM)
            return [to_all_rows(blocks[0])], blocks[1:]

        packed, blocks = stage(spread, *jobs[1])
        attended, mixed_own = [], []
        for number in range(last + 1):
            def work():
                done = attend(packed[number], parts[number])
                more = [to_all_rows(blocks[number])] if number < last else []
                back = [to_own_rows(attended[number - 1][0])] if number else []
                return done, more, back
            done, more, back = stage(work, *(jobs[number + 2] if number < 2 else []))
            attended.append(done)
            packed += more
            mixed_own += back
        if last == 0:
            stage(lambda: (), *jobs[3])
        mixed_own = stage(lambda: mixed_own + [to_own_rows(attended[-1][0])], *jobs[4])
        mixture = join_heads(mixed_own)
        halves = stage(lambda: both_halves(dot(mixture, out, ((1,), (1,)))), *jobs[5])
        hidden, normed_b = stage(
            lambda: norm(layer_in, gains[1], shifts[1], *halves), *jobs[6])
        up = finish_up()

        def expand():
            pre_act = dot(normed_b, up, ((1,), (0,)))
            return pre_act, jax.nn.gelu(pre_act).astype(BF16)

        pre_act, activated = stage(expand, *jobs[7])
        down = finish_down()
        own, far = stage(
            lambda: both_halves(dot(activated, down, ((1,), (1,)))), *jobs[8])
        layer_out = (hidden + own + far.astype(F32)).astype(BF16)
        saved = (layer_in, normed_a, packed, attended, mixture, hidden, normed_b, pre_act, activated)
        return layer_out, saved, attn + (up, down)

    def backward(layer, grad_branch, saved, norms, weights, jobs):
        gains, shifts = norms
        qkv, out, up, down = weights
        layer_in, normed_a, packed, attended, mixture, hidden, normed_b, pre_act, activated = saved

        def first():
            grad_act = dot(grad_branch, down, ((1,), (0,)))
            _, gelu_back = jax.vjp(jax.nn.gelu, pre_act)
            grad_pre = gelu_back(grad_act)[0].astype(BF16)
            grad_down = dot(grad_branch, activated, ((0,), (0,))).astype(BF16)
            return grad_pre, grad_down

        grad_pre, grad_down = stage(first, *jobs[0])

        def second():
            grad_second = both_halves(dot(grad_pre, up, ((1,), (1,))))
            return grad_second, dot(normed_b, grad_pre, ((0,), (0,))).astype(BF16)

        grad_second, grad_up = stage(second, *jobs[1])

        def third():
            grad_hidden, grad_attn, sums = norm_back(
                hidden, *grad_second, grad_branch, gains[1], True)
            grad_mixture = dot(grad_attn, out, ((1,), (0,))).astype(BF16)
            return grad_hidden, grad_attn, split_heads(grad_mixture, HEAD_DIM), sums

        late = hold(grad_down, *grad_second)
        grad_hidden, grad_attn, blocks, later = stage(
            third, ((DOWN, layer, SUM_1), lambda: reduce_dp(late, 1)), *jobs[2])
        after = hold(grad_down, grad_attn)
        grad_mixed, blocks = stage(
            lambda: ([to_all_rows(blocks[0])], blocks[1:]),
            ((DOWN, layer, SUM_0), lambda: reduce_dp(after, 0)), *jobs[3])
        grad_packed, returned, grad_out = [], [], None
        held_up = hold(grad_up, grad_mixed[0])

        def reduce_up():
            sent = reduce_dp(held_up, 1)
            return reduce_ctx(reduce_dp(held_up, 0), sent)


        for number in range(last + 1):
            if number:
                returned.append(to_own_rows(grad_packed[number - 1]))
            sent_back = returned[number - 1:] if number and layer == 0 else []

            def work():
                done = attend_back(packed[number], grad_mixed[number], attended[number][0],
                                   attended[number][1], parts[number])
                more = [to_all_rows(blocks[number])] if number < last else []
                extra = grad_out
                if number == 0:
                    extra = dot(grad_attn, mixture, ((0,), (0,))).astype(BF16)
                return done, more, extra, sent_back
            beside = jobs[5] if number == 1 else []
            if number == 0:
                beside = [
                    ((DOWN, layer, SUM), lambda: reduce_ctx(
                        held[DOWN, layer, SUM_0], held[DOWN, layer, SUM_1])),
                    ((UP, layer, SUM), reduce_up)] + list(jobs[4])
            done, more, grad_out, sent_back = stage(work, *beside)
            returned[len(returned) - len(sent_back):] = sent_back
            grad_packed.append(done)
            grad_mixed += more
        if last == 0:
            stage(lambda: (), *jobs[5])
        returned = stage(lambda: returned + [to_own_rows(grad_packed[-1])], *jobs[6])
        grad_proj = join_heads(returned)

        def fourth():
            grad_first = both_halves(dot(grad_proj, qkv, ((1,), (1,))))
            grad_qkv = dot(normed_a, grad_proj, ((0,), (0,))).astype(BF16)
            return grad_first, jnp.concatenate([grad_qkv, grad_out], 1)

        grad_first, grad_heads = stage(fourth, *jobs[7])

        def fifth():
            grad_input, early = norm_back(
                layer_in, *grad_first, grad_hidden, gains[0], False)
            return grad_input, jnp.stack([early[0], later[0], early[1], later[1]])

        heads_late = hold(grad_heads, *grad_first)
        grad_input, grad_norms = stage(
            fifth, ((ATTN, layer, SUM_1), lambda: reduce_dp(heads_late, 1)), *jobs[8])
        return grad_input, grad_norms, grad_heads

    def sum_norms(lower, upper):
        chosen = jnp.where(section == 0, lower, upper)
        if not square():
            total = lax.psum(chosen, (DP, CTX))
            place = lax.axis_index(DP) * contexts + ctx
            return lax.dynamic_slice_in_dim(total, place * own_rows, own_rows, 1)
        half = width // 2
        total = chosen[:, :half] + swap(chosen[:, half:], DP)
        return total[:, :own_rows] + swap(total[:, own_rows:], CTX)

    def entry_half(value):
        half = take(value.reshape(micro, 2, half_span, width), section, 1)
        return spread_tensor(reorder(half))

    def entry_rows(mine):
        other = swap(mine, SEC)
        return paired(mine[:, None], other[:, None], section, 1).reshape(count, width)

    def exit_rows(*values):
        halves = [take(value.reshape(tensors, 2, half_span, width), section, 1) for value in values]
        return spread_tensor(reorder(jnp.concatenate(halves, 1)))

    def place_layers(lower, upper):
        keep = jnp.where(section == 0, lower, upper)
        came = swap(jnp.where(section == 0, upper, lower), SEC)
        whole = paired(keep[:, None], came[:, None], section, 1)
        return whole.reshape(1, micro, 1, span, width)

    def own_layer(lower, upper):
        keep = jnp.where(section == 0, lower, upper)
        came = swap(jnp.where(section == 0, upper, lower), SEC)
        return paired(keep, came, section, 0)

    def reduce_tensor(blocks):
        return lax.psum_scatter(blocks, TEN, scatter_dimension=0)

    def reduce_direct(blocks):
        count, place = tensors, lax.axis_index(TEN)
        total = take(blocks, place).astype(F32)
        for step in range(1, count):
            pairs = [(n, (n + step) % count) for n in range(count)]
            sent = take(blocks, lax.rem(place + step, count))
            total = total + lax.ppermute(sent, TEN, pairs).astype(F32)
        return total

    def hidden_shares(value):
        return value.reshape(own_rows, tensors // 2, hidden_cols).transpose(1, 0, 2)

    def attn_shares(value):
        edge = value.shape[1] * qkv_cols // (qkv_cols + out_cols)
        if fast:
            cut = [shares_of_columns(value[:, :edge], 3 * HEAD_DIM),
                   shares_of_columns(value[:, edge:], HEAD_DIM)]
        else:
            cut = [piece.reshape(own_rows, tensors // 2, -1).transpose(1, 0, 2)
                   for piece in (value[:, :edge], value[:, edge:])]
        return jnp.concatenate(cut, 2)


    attn_both, entry, norms = stage(
        lambda: (over_tensor(attn_share), entry_half(inputs), gather_norms()))
    ffn_share = jnp.concatenate([w_up[0], rows_layout(w_down[0].T)], 1)
    norms_zero, norms_one = norms_of(0), norms_of(1)

    def start():
        held[ATTN, KEPT], held[ATTN, CAME] = attn_both[0], swap(attn_both[1], SEC)
        own = attn_layer(0)
        near = near_rows(own, True)
        full = all_rows(own, near, far_rows(own), far_rows(near))
        return entry_rows(entry), full, norms_zero, norms_one

    entries, attn_zero, norms_zero, norms_one = stage(start)
    cut_at = qkv_cols * tensors // 2

    def cut(full):
        return full[:, :cut_at], full[:, cut_at:]

    def ffn_begin():
        half, other = over_tensor(ffn_share)
        other = swap(other, SEC)
        made = {}
        for layer in range(2):
            mine = jnp.where(section == layer, half, other)
            made[UP, layer, OWN] = rows_layout(joined_columns(mine[:, :, :hidden_cols]))
            made[DOWN, layer, OWN] = rows_layout(joined_columns(mine[:, :, hidden_cols:]))
        return made

    def late(value):
        return hold(value, held[LAST])

    def near_job(what, layer, start=late):
        return (what, layer, NEAR), lambda: near_rows(start(held[what, layer, OWN]), what == ATTN)

    def same(value):
        return value

    def far_job(what, layer, state, start=late):
        return ((what, layer, OWN_FAR if state == OWN else NEAR_FAR),
                lambda: far_rows(start(held[what, layer, state])))

    def finish(what, layer):
        return lambda: all_rows(*[held.pop((what, layer, state))
                                  for state in (OWN, NEAR, OWN_FAR, NEAR_FAR)])

    out_zero, saved_zero, weights_zero = forward(
        entries, norms_zero, lambda: cut(attn_zero), finish(UP, 0), finish(DOWN, 0), [
            [],
            [(FFN, ffn_begin)],
            [near_job(UP, 0), far_job(UP, 0, OWN)],
            [far_job(UP, 0, NEAR), ((ATTN, 1, OWN), lambda: attn_layer(1))],
            [far_job(DOWN, 0, OWN), ((DOWN, 0, OWN), None), ((ATTN, 1, OWN), None)],
            [],
            [near_job(DOWN, 0, same), far_job(ATTN, 1, OWN, same)],
            [far_job(DOWN, 0, NEAR), near_job(ATTN, 1)],
            [],
        ])
    out_one, saved_one, weights_one = forward(
        out_zero, norms_one, lambda: cut(finish(ATTN, 1)()), finish(UP, 1), finish(DOWN, 1), [
            [far_job(ATTN, 1, NEAR, same)],
            [far_job(UP, 1, OWN)],
            [near_job(UP, 1), far_job(DOWN, 1, OWN), ((ENTRY, 1), lambda: entry_half(cotangent))],
            [far_job(UP, 1, NEAR)],
            [((DOWN, 1, OWN), None)],
            [],
            [near_job(DOWN, 1, same)],
            [far_job(DOWN, 1, NEAR)],
            [],
        ])
    top_grad = entry_rows(held.pop((ENTRY, 1)))
    grad_one, norm_sum_one, grad_heads_one = backward(
        1, top_grad, saved_one, norms_one, weights_one, [
            [], [], [], [],
            [((EXIT, 0), lambda: exit_rows(out_zero, out_one))],
            [], [], [], []])

    def all_shares(what):
        return (what, ALL), lambda: own_layer(hidden_shares(held.pop((what, 0, SUM))),
                                              hidden_shares(held.pop((what, 1, SUM))))

    def sum_shares(what):
        return (what, DONE), lambda: reduce_tensor(held.pop((what, ALL)))

    grad_zero, norm_sum_zero, grad_heads_zero = backward(
        0, grad_one, saved_zero, norms_zero, weights_zero, [
            [((ATTN, 1, SUM_0), lambda: reduce_dp(grad_heads_one, 0))],
            [],
            [((ATTN, 1, SUM), lambda: reduce_ctx(
                held[ATTN, 1, SUM_0], held[ATTN, 1, SUM_1], True))],
            [],
            [((EXIT, 2), lambda: exit_rows(grad_one))],
            [((DOWN, 0, SUM), None), ((UP, 0, SUM), None)],
            [all_shares(DOWN), all_shares(UP)],
            [],
            [sum_shares(DOWN)],
        ])

    def last_rows():
        sent = held[ATTN, 0, SUM_1]
        return (reduce_ctx(reduce_dp(grad_heads_zero, 0), sent, True),
                sum_norms(norm_sum_zero, norm_sum_one))

    def last_shares():
        return (own_layer(attn_shares(attn_zero_sum), attn_shares(held[ATTN, 1, SUM])),
                exit_rows(grad_zero), functools.reduce(jnp.add, tensor_pieces(norm_part)))

    attn_zero_sum, norm_part = stage(last_rows)
    attn_all, back_zero, norm_sums = stage(last_shares, sum_shares(UP))
    attn_total = reduce_direct(attn_all)
    layer_outputs = place_layers(held[EXIT, 0][:, :half_span], held[EXIT, 0][:, half_span:])
    boundary_grads = place_layers(back_zero, held[EXIT, 2])
    grad_down, grad_up = held[DOWN, DONE].astype(F32).T, held[UP, DONE].astype(F32)
    grad_qkv, grad_out = attn_total[:, :qkv_cols], attn_total[:, qkv_cols:]
    cut_list, place = [], 0
    for size in (parts if fast else [1] * share_heads):
        columns = size * 3 * HEAD_DIM
        cut_list.append(grad_qkv[:, place:place + columns].reshape(own_rows, 3, size, HEAD_DIM))
        place += columns
    grad_qkv = jnp.concatenate(cut_list, 2).transpose(1, 0, 2, 3).reshape(3, own_rows, -1)
    return (
        layer_outputs,
        boundary_grads,
        grad_qkv[None],
        grad_out.T[None],
        grad_up[None],
        grad_down[None],
        norm_sums[:2][None],
        norm_sums[2:][None],
    )


def solution(mesh):
    in_specs = (
        P(None, DP, (CTX, TEN), None),
        P(None, DP, (CTX, TEN), None),
        P(SEC, None, (DP, CTX), TEN),
        P(SEC, TEN, (DP, CTX)),
        P(SEC, (DP, CTX), TEN),
        P(SEC, TEN, (DP, CTX)),
        P(SEC, None, (DP, CTX)),
        P(SEC, None, (DP, CTX)),
    )
    out_specs = (
        P(SEC, None, DP, (CTX, TEN), None),
        P(SEC, None, DP, (CTX, TEN), None),
        P(SEC, None, (DP, CTX), TEN),
        P(SEC, TEN, (DP, CTX)),
        P(SEC, (DP, CTX), TEN),
        P(SEC, TEN, (DP, CTX)),
        P(SEC, None, (DP, CTX)),
        P(SEC, None, (DP, CTX)),
    )
    return jax.shard_map(
        per_device, mesh=mesh, in_specs=in_specs, out_specs=out_specs, check_vma=False
    )
```
